128 devices in a mesh: gx: 4 (over x), gy: 4 (over z), gz: 8 (over y, core).
Axes of the slice: x: 4, y: 4, z: 4, core: 2. Of those that a mesh axis runs over, the one named last changes fastest.
Arguments:
- fields: float32 [24, 32, 128, 1024], P(None, 'gx', 'gy', 'gz'), may hold values from -8.5 to 8.5
- velocity: float32 [3, 32, 128, 1024], P(None, 'gx', 'gy', 'gz'), may hold values from -0.4 to 0.4
- diffusivity: float32 [24], replicated, may hold values from 0.02 to 0.15
- weight_in: bfloat16 [24, 1600], replicated, may hold values from -1.25 to 1.25
- bias_in: float32 [1600], replicated, may hold values from -3 to 3
- weight_mid: bfloat16 [1600, 800], replicated, may hold values from -0.15625 to 0.15625
- bias_mid: float32 [800], replicated, may hold values from -3 to 3
- weight_low: bfloat16 [800, 400], replicated, may hold values from -0.21875 to 0.21875
- bias_low: float32 [400], replicated, may hold values from -3 to 3
- weight_out: bfloat16 [400, 24], replicated, may hold values from -0.3125 to 0.3125
- bias_out: float32 [24], replicated, may hold values from -3 to 3
- react_list: int32 [128, 96], P(('gx', 'gy', 'gz')), may hold values from -1 to 255, as said below
- owner_table: int32 [128, 96], P(('gx', 'gy', 'gz')), may hold values from -1 to 127, as said below
Outputs:
- updated: float32 [24, 32, 128, 1024], P(None, 'gx', 'gy', 'gz')
- owner_activity: float32 [128], P(('gx', 'gy', 'gz'))
The draws below stay inside these ranges and needn't reach their ends.
Inputs may be any that keep to these rules, and one draw needn't show every extreme that they name: `react_list`: row d lists distinct blocks of brick d, valid entries first and -1 after them; a brick lists at most 96 blocks and some brick lists exactly 96; all bricks together list 32 times the number of devices. owner_table[d, i] is -1 exactly where react_list[d, i] is, else the owner's index over gx+gy+gz; every device owns exactly 32 blocks; no brick sends more than 1 block to one owner, and some brick sends exactly 1 to some owner.
All inputs are finite; a program needn't handle non-finite values.
Results may differ from the reference program's by a relative error of at most 0.00058.
Values may be sent and summed in bfloat16 or wider, within the bound.
No kernel may reach another device: no remote copies, remote signals or barrier semaphores. Data moves between devices by JAX's collectives and lax.ppermute only.
A program may use at most 256 MiB of HBM per device.

```python
import math
import jax
import jax.numpy as jnp
from jax import lax

FIELDS = 24
HID_ONE = 1600
HID_TWO = 800
HID_THREE = 400
CX = 8
CY = 32
CZ = 128
OWNED = 32
LIST_MAX = 96
NX = 32
NY = 128
NZ = 1024
N_GX = 4
N_GY = 4
N_GZ = 8
DEVICES = 128


def draw_fields(key, part):
    base_key = jax.random.fold_in(key, 11)
    key_scale, key_values = jax.random.split(base_key, 2)
    column_scale = jnp.exp(jax.random.uniform(key_scale, (FIELDS, NX, NY, 1), jnp.float32, jnp.log(0.5), jnp.log(2.0)))
    rough = jnp.clip(jax.random.normal(key_values, (FIELDS, NX, NY, NZ), jnp.float32), -4.0, 4.0)
    return (rough * column_scale).astype(jnp.float32)


def layout(key):
    base_key = jax.random.fold_in(key, 5)
    key_first, key_second, key_place, key_blocks, key_owner = jax.random.split(base_key, 5)
    groups = DEVICES // 4
    spare_blocks = 4 * OWNED - LIST_MAX
    first_share = jax.random.randint(key_first, (groups,), 0, spare_blocks + 1)
    second_share = jax.random.randint(key_second, (groups,), 0, 1 << 20) % (spare_blocks - first_share + 1)
    third_share = spare_blocks - first_share - second_share
    pattern = jnp.stack([jnp.full((groups,), LIST_MAX, jnp.int32), first_share, second_share, third_share], axis=1).reshape(-1).astype(jnp.int32)
    placing = jax.random.permutation(key_place, DEVICES)
    counts = jnp.zeros((DEVICES,), jnp.int32).at[placing].set(pattern)
    block_count = CX * CY
    scores = jax.random.randint(key_blocks, (DEVICES, block_count), 0, 1 << 20) * block_count + jnp.arange(block_count, dtype=jnp.int32)[None, :]
    chosen = jnp.argsort(scores, axis=1)[:, :LIST_MAX].astype(jnp.int32)
    positions = jnp.arange(LIST_MAX, dtype=jnp.int32)[None, :]
    present = positions < counts[:, None]
    starting = jnp.cumsum(counts) - counts
    serial = starting[:, None] + positions
    owners = jax.random.permutation(key_owner, DEVICES).astype(jnp.int32)[serial % DEVICES]
    return (jnp.where(present, chosen, -1).astype(jnp.int32), jnp.where(present, owners, -1).astype(jnp.int32))


def draw_react_list(key, part):
    return layout(key)[0]


def draw_owner_table(key, part):
    return layout(key)[1]


def shard_levels(rng, dims, shards, least, high):
    factor_of = 1.0
    for dim, parts in shards:
        heights = jax.random.uniform(jax.random.fold_in(jax.random.fold_in(rng, 6), dim), (parts,), jnp.float32, least / len(shards), high / len(shards))
        factor_of = factor_of * jnp.repeat(jnp.exp(heights), dims[dim] // parts).reshape((-1,) + (1,) * (len(dims) - 1 - dim))
    return factor_of


def bell_draw(stream_key, extent, deviation, reach, held_as=jnp.bfloat16):
    return jnp.clip(deviation * jax.random.normal(stream_key, extent, jnp.float32), -reach, reach).astype(held_as)


def setup_inputs(seed: int = 0) -> dict:
    key_list = jax.random.split(jax.random.key(seed), 14)
    fields = draw_fields(jax.random.fold_in(key_list[13], 71), 0)
    velocity = jnp.clip(jax.random.uniform(key_list[1], (3, NX, NY, NZ), jnp.float32, -0.4, 0.4) * shard_levels(key_list[1], (3, NX, NY, NZ), ((1, 4), (2, 4), (3, 8)), -0.4, 0.0), -0.4, 0.4)
    diffusivity = jnp.clip(jnp.exp(jax.random.uniform(key_list[2], (FIELDS,), jnp.float32, math.log(0.02), math.log(0.15))), 0.02, 0.15)
    weight_in = bell_draw(key_list[3], (FIELDS, HID_ONE), FIELDS ** -0.5, 1.25)
    bias_in = bell_draw(key_list[4], (HID_ONE,), 0.5, 3.0, jnp.float32)
    weight_mid = bell_draw(key_list[5], (HID_ONE, HID_TWO), HID_ONE ** -0.5, 0.15625)
    bias_mid = bell_draw(key_list[6], (HID_TWO,), 0.5, 3.0, jnp.float32)
    weight_low = bell_draw(key_list[7], (HID_TWO, HID_THREE), HID_TWO ** -0.5, 0.21875)
    bias_low = bell_draw(key_list[8], (HID_THREE,), 0.5, 3.0, jnp.float32)
    weight_out = bell_draw(key_list[9], (HID_THREE, FIELDS), HID_THREE ** -0.5, 0.3125)
    bias_out = bell_draw(key_list[10], (FIELDS,), 0.5, 3.0, jnp.float32)
    react_list = draw_react_list(jax.random.fold_in(key_list[13], 71), 0)
    owner_table = draw_owner_table(jax.random.fold_in(key_list[13], 71), 0)
    return {"fields": fields, "velocity": velocity, "diffusivity": diffusivity, "weight_in": weight_in, "bias_in": bias_in, "weight_mid": weight_mid, "bias_mid": bias_mid, "weight_low": weight_low, "bias_low": bias_low, "weight_out": weight_out, "bias_out": bias_out, "react_list": react_list, "owner_table": owner_table}


viscous = 0.05
third_part = 1.0 / 3.0


def laplace(values_in):
    summed = -6.0 * values_in
    for axis_dim in (1, 2, 3):
        summed = summed + jnp.roll(values_in, -1, axis_dim) + jnp.roll(values_in, 1, axis_dim)
    return summed


def transport(values_in, speeds):
    spread = -6.0 * values_in
    flux_sum = jnp.zeros_like(values_in)
    for axis_dim in (1, 2, 3):
        carried = speeds[axis_dim - 1][None] * values_in
        flux_sum = flux_sum + 0.5 * (jnp.roll(carried, -1, axis_dim) - jnp.roll(carried, 1, axis_dim))
        spread = spread + jnp.roll(values_in, -1, axis_dim) + jnp.roll(values_in, 1, axis_dim)
    return viscous * spread - flux_sum


def network(cell_rows, weight_in, bias_in, weight_mid, bias_mid, weight_low, bias_low, weight_out, bias_out):
    hidden = jax.nn.silu(jnp.dot(cell_rows, weight_in, preferred_element_type=jnp.float32) + bias_in).astype(jnp.bfloat16)
    hidden = jax.nn.silu(jnp.dot(hidden, weight_mid, preferred_element_type=jnp.float32) + bias_mid).astype(jnp.bfloat16)
    hidden = jax.nn.silu(jnp.dot(hidden, weight_low, preferred_element_type=jnp.float32) + bias_low).astype(jnp.bfloat16)
    return jnp.dot(hidden, weight_out, preferred_element_type=jnp.float32) + bias_out


def reference(fields, velocity, diffusivity, weight_in, bias_in, weight_mid, bias_mid, weight_low, bias_low, weight_out, bias_out, react_list, owner_table):
    section_one = fields + transport(fields, velocity)
    section_two = 0.75 * fields + 0.25 * (section_one + transport(section_one, velocity))
    flowed = third_part * fields + (2.0 / 3.0) * (section_two + transport(section_two, velocity))

    devices = N_GX * N_GY * N_GZ
    device = jnp.arange(devices, dtype=jnp.int32)[:, None]
    brick_x = device // (N_GY * N_GZ)
    brick_y = (device // N_GZ) % N_GY
    brick_z = device % N_GZ
    present = react_list >= 0
    clipped = jnp.where(present, react_list, 0).astype(jnp.int32)
    column_x = (brick_x * CX + clipped // CY).reshape(-1).astype(jnp.int32)
    column_y = (brick_y * CY + clipped % CY).reshape(-1).astype(jnp.int32)
    column_z = jnp.broadcast_to(brick_z * CZ, react_list.shape).reshape(-1).astype(jnp.int32)
    ordering = jnp.argsort(jnp.where(present, 0, 1).reshape(-1).astype(jnp.int32), stable=True)[: devices * OWNED]
    column_x = column_x[ordering]
    column_y = column_y[ordering]
    column_z = column_z[ordering]
    owners = owner_table.reshape(-1)[ordering].astype(jnp.int32)

    def fetch_block(start_x, start_y, start_z):
        piece = lax.dynamic_slice(flowed, (jnp.int32(0), start_x, start_y, start_z), (FIELDS, 1, 1, CZ))
        return piece.reshape(FIELDS, CZ)

    blocks = jax.vmap(fetch_block)(column_x, column_y, column_z)
    cell_rows = blocks.astype(jnp.bfloat16).transpose(0, 2, 1).reshape(devices, OWNED * CZ, FIELDS)

    def run_owner(portion):
        return network(portion, weight_in, bias_in, weight_mid, bias_mid, weight_low, bias_low, weight_out, bias_out)

    increments = lax.map(run_owner, cell_rows)
    increments = increments.reshape(devices * OWNED, CZ, FIELDS).transpose(0, 2, 1)
    block_heat = jnp.mean(increments[:, 0, :] ** 2, axis=-1)
    owner_activity = jax.ops.segment_sum(block_heat, owners, num_segments=devices) / 8.0

    offsets = column_z[:, None] + jnp.arange(CZ, dtype=jnp.int32)[None, :]
    reacted = flowed.at[:, column_x[:, None], column_y[:, None], offsets].add(increments.transpose(1, 0, 2))
    updated = reacted + diffusivity[:, None, None, None] * laplace(reacted)
    return updated, owner_activity
```

```python
import math

import jax
import jax.numpy as jnp
from jax import lax
from jax.sharding import PartitionSpec as P

OWNED = 32


viscous = 0.05
third_part = 1.0 / 3.0


def extended(value, sides, width):
    edges = {}
    for axis, dim in sides:
        devices, length = (lax.axis_size(axis), value.shape[dim])
        up = [(i, (i + 1) % devices) for i in range(devices)]
        last = lax.slice_in_dim(value, length - width, length, axis=dim)
        leading = lax.slice_in_dim(value, 0, width, axis=dim)
        edges[dim] = (
            lax.ppermute(last, axis, up),
            lax.ppermute(leading, axis, [(b, a) for a, b in up]),
        )
    done = []
    for _, dim in sides:
        low, high = edges[dim]
        around = [(width, width) if d in done else (0, 0) for d in range(value.ndim)]
        value = jnp.concatenate([jnp.pad(low, around), value, jnp.pad(high, around)], axis=dim)
        done.append(dim)
    return value


def split_up(value, dim, devices):
    dims = value.shape
    tiles = value.reshape(*dims[:dim], devices, dims[dim] // devices, *dims[dim + 1 :])
    return jnp.moveaxis(tiles, dim, 0)


def joined_along(tiles, dim):
    dims = list(tiles.shape[1:])
    dims[dim] *= tiles.shape[0]
    return jnp.moveaxis(tiles, 0, dim).reshape(dims)


def one_exchange(value, axis, axes, splits, concats):
    sizes = [lax.axis_size(a) for a in axes]
    tiles = split_up(value, splits[0], sizes[0])
    tiles = jnp.moveaxis(split_up(tiles, splits[1] + 1, sizes[1]), 0, 1)
    inside = tiles.shape[2:]
    tiles = tiles.reshape(-1, *inside)
    tiles = lax.all_to_all(tiles, axis, split_axis=0, concat_axis=0, tiled=True)
    tiles = joined_along(tiles.reshape(*sizes, *inside), concats[0] + 1)
    return joined_along(tiles, concats[1])


def pad_cells(array):
    return extended(array, (("gx", 1), ("gy", 2), ("gz", 3)), 1)


def interior(padded, axis_dim, offset):
    window = [slice(None)] + [slice(1, -1)] * 3
    window[axis_dim] = slice(1 + offset, padded.shape[axis_dim] - 1 + offset)
    return padded[tuple(window)]


def laplace(padded):
    summed = -6.0 * interior(padded, 1, 0)
    for axis_dim in (1, 2, 3):
        summed = summed + interior(padded, axis_dim, 1) + interior(padded, axis_dim, -1)
    return summed


def transport(padded, speeds):
    centre = interior(padded, 1, 0)
    spread = -6.0 * centre
    flux_sum = jnp.zeros_like(centre)
    for axis_dim in (1, 2, 3):
        carried = speeds[axis_dim - 1][None] * padded
        flux_sum = flux_sum + 0.5 * (
            interior(carried, axis_dim, 1) - interior(carried, axis_dim, -1)
        )
        spread = spread + interior(padded, axis_dim, 1) + interior(padded, axis_dim, -1)
    return viscous * spread - flux_sum


def network(
    block_in, weight_in, bias_in, weight_mid, bias_mid, weight_low, bias_low, weight_out, bias_out
):
    hidden = jnp.einsum("bfz,fh->bhz", block_in, weight_in, preferred_element_type=jnp.float32)
    hidden = jax.nn.silu(hidden + bias_in[None, :, None]).astype(jnp.bfloat16)
    hidden = jnp.einsum("bhz,hk->bkz", hidden, weight_mid, preferred_element_type=jnp.float32)
    hidden = jax.nn.silu(hidden + bias_mid[None, :, None]).astype(jnp.bfloat16)
    hidden = jnp.einsum("bkz,kl->blz", hidden, weight_low, preferred_element_type=jnp.float32)
    hidden = jax.nn.silu(hidden + bias_low[None, :, None]).astype(jnp.bfloat16)
    result = jnp.einsum("blz,lf->bfz", hidden, weight_out, preferred_element_type=jnp.float32)
    return result + bias_out[None, :, None]


def local(
    fields,
    velocity,
    diffusivity,
    weight_in,
    bias_in,
    weight_mid,
    bias_mid,
    weight_low,
    bias_low,
    weight_out,
    bias_out,
    react_list,
    owner_table,
):
    field_count, cells_x, cells_y, cells_z = fields.shape
    padded = pad_cells(jnp.concatenate([fields, velocity], axis=0))
    speeds = padded[field_count:]
    section_one = fields + transport(padded[:field_count], speeds)
    section_two = 0.75 * fields + 0.25 * (section_one + transport(pad_cells(section_one), speeds))
    flowed = third_part * fields + 2.0 / 3.0 * (
        section_two + transport(pad_cells(section_two), speeds)
    )
    devices = lax.axis_size(("gx", "gy", "gz"))
    block_ids = react_list[0]
    owners = owner_table[0]
    listed = block_ids.shape[0]
    capacity = (listed + devices - 1) // devices
    slots_all = devices * capacity
    block_count = cells_x * cells_y
    present = block_ids >= 0
    positions = jnp.arange(listed, dtype=jnp.int32)
    earlier = (
        (owners[None, :] == owners[:, None])
        & present[None, :]
        & (positions[None, :] < positions[:, None])
    )
    earlier_count = jnp.sum(earlier.astype(jnp.int32), axis=1)
    target_slot = jnp.where(present, owners * capacity + earlier_count, -1)
    slot_hot = (target_slot[None, :] == jnp.arange(slots_all, dtype=jnp.int32)[:, None]).astype(
        jnp.float32
    )
    block_hot = (block_ids[:, None] == jnp.arange(block_count, dtype=jnp.int32)[None, :]).astype(
        jnp.float32
    )
    routing_table = jnp.dot(slot_hot, block_hot, precision=lax.Precision.HIGHEST)
    slot_mask = (jnp.sum(slot_hot, axis=1) > 0.5).astype(jnp.int32)
    brick_blocks = flowed.reshape(field_count, block_count, cells_z).astype(jnp.bfloat16)
    outgoing = jnp.einsum(
        "sb,fbz->sfz",
        routing_table.astype(jnp.bfloat16),
        brick_blocks,
        preferred_element_type=jnp.float32,
    ).astype(jnp.bfloat16)
    outgoing = outgoing.reshape(devices, capacity, field_count, cells_z)
    slot_mask = slot_mask.reshape(devices, capacity)
    plane_count = lax.axis_size("gx") * lax.axis_size("gy")
    depth_count = lax.axis_size("gz")
    arrived, arrived_mask = (
        one_exchange(
            outgoing.reshape(plane_count, depth_count, capacity, field_count, cells_z),
            ("gx", "gy", "gz"),
            (("gx", "gy"), "gz"),
            (0, 1),
            (0, 1),
        ),
        one_exchange(
            slot_mask.reshape(plane_count, depth_count, capacity),
            ("gx", "gy", "gz"),
            (("gx", "gy"), "gz"),
            (0, 1),
            (0, 1),
        ),
    )
    arrived = arrived.reshape(slots_all, field_count, cells_z)
    occupied = arrived_mask.reshape(slots_all)
    slot_numbers = jnp.arange(slots_all, dtype=jnp.int32)
    position = (
        jnp.sum(jnp.where(slot_numbers[None, :] <= slot_numbers[:, None], occupied[None, :], 0), axis=1) - 1
    )
    selector = (
        (position[None, :] == jnp.arange(OWNED, dtype=jnp.int32)[:, None])
        & (occupied[None, :] == 1)
    ).astype(jnp.float32)
    compact = jnp.einsum(
        "rs,sfz->rfz", selector.astype(jnp.bfloat16), arrived, preferred_element_type=jnp.float32
    ).astype(jnp.bfloat16)
    group_size = math.gcd(OWNED, 8)

    def run_group(blockset):
        return network(
            blockset,
            weight_in,
            bias_in,
            weight_mid,
            bias_mid,
            weight_low,
            bias_low,
            weight_out,
            bias_out,
        )

    chemistry = lax.map(
        run_group, compact.reshape(OWNED // group_size, group_size, field_count, cells_z)
    )
    chemistry = chemistry.reshape(OWNED, field_count, cells_z)
    owner_activity = (jnp.sum(jnp.mean(chemistry[:, 0, :] ** 2, axis=-1)) / 8.0).reshape(1)
    returning = jnp.einsum("rs,rfz->sfz", selector, chemistry, precision=lax.Precision.HIGHEST)
    returning = returning.reshape(devices, capacity, field_count, cells_z)
    plane_count = lax.axis_size("gx") * lax.axis_size("gy")
    depth_count = lax.axis_size("gz")
    came_back = one_exchange(
        returning.reshape(plane_count, depth_count, capacity, field_count, cells_z),
        ("gx", "gy", "gz"),
        (("gx", "gy"), "gz"),
        (0, 1),
        (0, 1),
    )
    came_back = came_back.reshape(slots_all, field_count, cells_z)
    added = jnp.einsum("sb,sfz->fbz", routing_table, came_back, precision=lax.Precision.HIGHEST)
    added = added.reshape(field_count, cells_x, cells_y, cells_z)
    reacted = flowed + added
    rates = diffusivity[:, None, None, None]
    updated = reacted + rates * laplace(pad_cells(reacted))
    return (updated, owner_activity)


def solution(mesh):
    return jax.shard_map(
        local,
        mesh=mesh,
        in_specs=(
            P(None, "gx", "gy", "gz"),
            P(None, "gx", "gy", "gz"),
            P(),
            P(),
            P(),
            P(),
            P(),
            P(),
            P(),
            P(),
            P(),
            P(("gx", "gy", "gz"), None),
            P(("gx", "gy", "gz"), None),
        ),
        out_specs=(P(None, "gx", "gy", "gz"), P(("gx", "gy", "gz"))),
        check_vma=False,
    )
```

```python
import functools

import jax
import jax.numpy as jnp
from jax import lax
from jax.experimental import pallas as pl
from jax.experimental.pallas import tpu as pltpu
from jax.sharding import PartitionSpec as P

OWNED = 32
GROUP = 4
ALL = ("gx", "gy", "gz")
F32, BF16 = jnp.float32, jnp.bfloat16
TN = (((0,), (0,)), ((), ()))
NT = (((1,), (1,)), ((), ()))


def one_hot_ends():
    rows = lax.broadcasted_iota(jnp.int32, (16, 128), 0)
    lanes = lax.broadcasted_iota(jnp.int32, (16, 128), 1)
    return (((rows == 0) & (lanes == 0)) | ((rows == 1) & (lanes == 127))).astype(F32).astype(BF16)


def z_columns(low, high):
    rows = lax.broadcasted_iota(jnp.int32, (16, 256), 0)
    pair = jnp.where(rows == 0, low, jnp.where(rows == 1, high, 0.0)).astype(BF16)
    return lax.dot_general(pair, one_hot_ends(), TN, preferred_element_type=F32)


def z_ends(cells):
    return lax.dot_general(one_hot_ends(), cells.astype(BF16), NT, preferred_element_type=F32)


def shifted(centre, y_low, y_high, z_col):
    rows = lax.broadcasted_iota(jnp.int32, (32, 128), 0)
    lanes = lax.broadcasted_iota(jnp.int32, (32, 128), 1)
    y_next = jnp.where(rows == 31, y_high, pltpu.roll(centre, 31, 0))
    y_prev = jnp.where(rows == 0, y_low, pltpu.roll(centre, 1, 0))
    z_next = jnp.where(lanes == 127, z_col, pltpu.roll(centre, 127, 1))
    z_prev = jnp.where(lanes == 0, z_col, pltpu.roll(centre, 1, 1))
    return y_next, y_prev, z_next, z_prev


def put_faces(new, f, x, xf, xl, yf, yl):
    if x == 0:
        xf[f] = new.astype(BF16)
    if x == 7:
        xl[f] = new.astype(BF16)
    yf[f, x : x + 1] = new[0:1]
    yl[f, x : x + 1] = new[31:32]


def put_z_faces(out, f, zf, zl):
    ends = z_ends(out[f].reshape(256, 128))
    zf[f] = ends[0:1]
    zl[f] = ends[1:2]


CODE_UNIT = 32.0
CODE_SCALE = 32767.0 / 38.0 / 0.6931471805599453


def coded(value):
    level = (jnp.log(1.0 + CODE_UNIT * jnp.abs(value)) * CODE_SCALE + 0.5).astype(jnp.int32)
    return jnp.where(value < 0.0, -level, level).astype(jnp.int16)


def decoded(code):
    level = code.astype(jnp.int32).astype(F32)
    size = (jnp.exp(jnp.abs(level) * (1.0 / CODE_SCALE)) - 1.0) * (1.0 / CODE_UNIT)
    return jnp.where(level < 0.0, -size, size)


def prep_kernel(fields, velocity, xf, xl, yf, yl, zf, zl):
    def put(ref, i, f):
        xf[f] = ref[i, 0].astype(BF16)
        xl[f] = ref[i, 7].astype(BF16)
        for x in range(8):
            yf[f, x : x + 1] = ref[i, x, 0:1]
            yl[f, x : x + 1] = ref[i, x, 31:32]
        ends = z_ends(ref[i].reshape(256, 128))
        zf[f] = ends[0:1]
        zl[f] = ends[1:2]

    for f in range(24):
        put(fields, f, f)
    xf[24] = velocity[0, 0].astype(BF16)
    xl[24] = velocity[0, 7].astype(BF16)
    for x in range(8):
        yf[24, x : x + 1] = velocity[1, x, 0:1]
        yl[24, x : x + 1] = velocity[1, x, 31:32]
    ends = z_ends(velocity[2].reshape(256, 128))
    zf[24] = ends[0:1]
    zl[24] = ends[1:2]


def section_kernel(kind, *refs):
    refs = list(refs)
    q = refs.pop(0)
    start = q if kind == 1 else refs.pop(0)
    xlo, xhi, ylo, yhi, zlo, zhi = refs[:6]
    del refs[:6]
    if kind == 1:
        velocity, vxlo, vxhi, vylo, vyhi, vzlo, vzhi = refs[:7]
        del refs[:7]
    else:
        coef = refs.pop(0)
    if kind == 3:
        routing = refs.pop(0)
    out = refs.pop(0)
    if kind == 1:
        coef = refs.pop(0)
    if kind < 3:
        xf, xl, yf, yl, zf, zl = refs[:6]
        del refs[:6]
    else:
        outgoing = refs.pop(0)
    zcol = refs.pop(0)

    if kind == 1:

        @pl.when(pl.program_id(0) == 0)
        def _():
            zcol[0] = z_columns(vzlo[0], vzhi[0])
            for x in range(8):
                before = vxlo[0].astype(F32) if x == 0 else velocity[0, x - 1]
                after = vxhi[0].astype(F32) if x == 7 else velocity[0, x + 1]
                y_next, y_prev, _, _ = shifted(
                    velocity[1, x], vylo[0, x : x + 1], vyhi[0, x : x + 1], velocity[1, x]
                )
                _, _, z_next, z_prev = shifted(
                    velocity[2, x], vylo[0, x : x + 1], vyhi[0, x : x + 1], zcol[0, 32 * x : 32 * x + 32]
                )
                coef[0, x] = 0.05 - 0.5 * after
                coef[1, x] = 0.05 + 0.5 * before
                coef[2, x] = 0.05 - 0.5 * y_next
                coef[3, x] = 0.05 + 0.5 * y_prev
                coef[4, x] = 0.05 - 0.5 * z_next
                coef[5, x] = 0.05 + 0.5 * z_prev

    for f in range(GROUP):
        zcol[f] = z_columns(zlo[f], zhi[f])
    for x in range(8):
        ce = [coef[i, x] for i in range(6)]
        for f in range(GROUP):
            centre = q[f, x]
            before = xlo[f].astype(F32) if x == 0 else q[f, x - 1]
            after = xhi[f].astype(F32) if x == 7 else q[f, x + 1]
            y_next, y_prev, z_next, z_prev = shifted(
                centre, ylo[f, x : x + 1], yhi[f, x : x + 1], zcol[f, 32 * x : 32 * x + 32]
            )
            moved = (
                0.7 * centre
                + (ce[0] * after + ce[1] * before)
                + (ce[2] * y_next + ce[3] * y_prev)
                + (ce[4] * z_next + ce[5] * z_prev)
            )
            if kind == 1:
                new = moved
            elif kind == 2:
                new = 0.75 * start[f, x] + 0.25 * moved
            else:
                new = (1.0 / 3.0) * start[f, x] + (2.0 / 3.0) * moved
            out[f, x] = new
            if kind < 3:
                put_faces(new, f, x, xf, xl, yf, yl)
    for f in range(GROUP):
        if kind < 3:
            put_z_faces(out, f, zf, zl)
        else:
            blocks = out[f].reshape(256, 128).astype(BF16)
            outgoing[:, 128 * f : 128 * f + 128] = jnp.dot(
                routing[...], blocks, preferred_element_type=F32
            ).astype(BF16)


def react_kernel(flowed, back, table, out, xf, xl, yf, yl, zf, zl):
    for f in range(GROUP):
        value = decoded(back[:, 128 * f : 128 * f + 128])
        coarse = value.astype(BF16)
        rest = (value - coarse.astype(F32)).astype(BF16)
        added = jnp.dot(table[...], coarse, preferred_element_type=F32)
        added += jnp.dot(table[...], rest, preferred_element_type=F32)
        for x in range(8):
            new = flowed[f, x] + added[32 * x : 32 * x + 32]
            out[f, x] = new
            put_faces(new, f, x, xf, xl, yf, yl)
        put_z_faces(out, f, zf, zl)


def diffuse_kernel(rates, q, xlo, xhi, ylo, yhi, zlo, zhi, out, zcol):
    base = pl.program_id(0) * GROUP
    for f in range(GROUP):
        zcol[f] = z_columns(zlo[f], zhi[f])
        rate = rates[base + f]
        for x in range(8):
            centre = q[f, x]
            before = xlo[f].astype(F32) if x == 0 else q[f, x - 1]
            after = xhi[f].astype(F32) if x == 7 else q[f, x + 1]
            y_next, y_prev, z_next, z_prev = shifted(
                centre, ylo[f, x : x + 1], yhi[f, x : x + 1], zcol[f, 32 * x : 32 * x + 32]
            )
            spread = (after + before) + (y_next + y_prev) + (z_next + z_prev) - 6.0 * centre
            out[f, x] = centre + rate * spread


def network_kernel(slots, arrived, w1, b1, w2, b2, w3, b3, w4, b4, out, heat):
    step = pl.program_id(0)

    @pl.when(step == 0)
    def _():
        out[...] = jnp.zeros_like(out)
        heat[...] = jnp.zeros_like(heat)

    def activated(weights, bias, cells):
        half = jnp.dot(weights[...], cells, preferred_element_type=F32)
        half = half + jnp.concatenate([bias[...], bias[...]], axis=1)
        return (half + half * jnp.tanh(half)).astype(BF16)

    first, second = slots[2 * step], slots[2 * step + 1]
    cells = jnp.concatenate([arrived[first], arrived[second]], axis=1)
    hidden = activated(w1, b1, cells)
    hidden = activated(w2, b2, hidden)
    hidden = activated(w3, b3, hidden)
    result = jnp.dot(w4[...], hidden, preferred_element_type=F32)
    result = result + jnp.concatenate([b4[...], b4[...]], axis=1)
    codes = coded(result)
    out[first] = codes[:, :128]
    out[second] = codes[:, 128:]
    squares = result[0:8] * result[0:8]
    heat[...] += squares[:, :128] + squares[:, 128:]


def params(mib):
    return pltpu.CompilerParams(vmem_limit_bytes=mib * 1024 * 1024)


def sds(shape, dtype):
    return jax.ShapeDtypeStruct(shape, dtype)


def whole(shape):
    return pl.BlockSpec(shape, lambda *_: (0,) * len(shape))


def at(shape, place):
    return pl.BlockSpec(shape, lambda *_: place)


BRICK = pl.BlockSpec((GROUP, 8, 32, 128), lambda g, *_: (g, 0, 0, 0))
X_FACE = pl.BlockSpec((GROUP, 32, 128), lambda g, *_: (g, 0, 0))
Y_FACE = pl.BlockSpec((GROUP, 8, 128), lambda g, *_: (g, 0, 0))
Z_FACE = pl.BlockSpec((GROUP, 1, 256), lambda g, *_: (g, 0, 0))
FACES = [X_FACE, X_FACE, Y_FACE, Y_FACE, Z_FACE, Z_FACE]
SLOTS = pl.BlockSpec((128, GROUP * 128), lambda g, *_: (0, g))


def face_shapes(count):
    return [
        sds((count, 32, 128), BF16),
        sds((count, 32, 128), BF16),
        sds((count, 8, 128), F32),
        sds((count, 8, 128), F32),
        sds((count, 1, 256), F32),
        sds((count, 1, 256), F32),
    ]


def exchange(faces):
    got = []
    for axis, first, last in zip(ALL, faces[0::2], faces[1::2]):
        n = lax.axis_size(axis)
        got.append(lax.ppermute(last, axis, [(i, (i + 1) % n) for i in range(n)]))
        got.append(lax.ppermute(first, axis, [((i + 1) % n, i) for i in range(n)]))
    return got


def section(kind, args, in_specs, out_shapes, out_specs):
    return pl.pallas_call(
        functools.partial(section_kernel, kind),
        grid=(24 // GROUP,),
        in_specs=in_specs,
        out_specs=out_specs,
        out_shape=out_shapes,
        scratch_shapes=[pltpu.VMEM((GROUP, 256, 128), F32)],
        compiler_params=params(24),
    )(*args)


def swap(tiles):
    return lax.all_to_all(tiles, ALL, split_axis=0, concat_axis=0, tiled=True)


def local(
    fields,
    velocity,
    diffusivity,
    weight_in,
    bias_in,
    weight_mid,
    bias_mid,
    weight_low,
    bias_low,
    weight_out,
    bias_out,
    react_list,
    owner_table,
):
    brick = sds(fields.shape, F32)
    ids, owners = react_list[0], owner_table[0]
    everyone = lax.all_gather(owner_table, ALL, axis=0, tiled=True)
    me = lax.axis_index(ALL)
    sends = jnp.any(everyone == me, axis=1)
    numbers = jnp.arange(128, dtype=jnp.int32)
    rank = jnp.sum(jnp.where((numbers[None, :] < numbers[:, None]) & sends[None, :], 1, 0), axis=1)
    slots = jnp.sum(
        jnp.where((rank[None, :] == numbers[:OWNED, None]) & sends[None, :], numbers[None, :], 0), axis=1
    ).astype(jnp.int32)
    slot_hot = (owners[None, :] == numbers[:, None]).astype(BF16)
    block_hot = (ids[:, None] == jnp.arange(256, dtype=jnp.int32)[None, :]).astype(BF16)
    routing = jnp.dot(slot_hot, block_hot, preferred_element_type=F32).astype(BF16)
    table = lax.dot_general(block_hot, slot_hot, (((0,), (1,)), ((), ())), preferred_element_type=F32).astype(BF16)

    half = jnp.asarray(0.5, BF16)
    w1, w2, w3, w4 = (weight_in * half).T, (weight_mid * half).T, (weight_low * half).T, weight_out.T
    b1, b2, b3, b4 = (
        jnp.broadcast_to((s * b)[:, None], (b.shape[0], 128))
        for s, b in ((0.5, bias_in), (0.5, bias_mid), (0.5, bias_low), (1.0, bias_out))
    )

    faces = pl.pallas_call(
        prep_kernel, out_shape=face_shapes(25), compiler_params=params(24)
    )(fields, velocity)
    halo = exchange(faces)
    own_halo = [
        at((1, 32, 128), (24, 0, 0)),
        at((1, 32, 128), (24, 0, 0)),
        at((1, 8, 128), (24, 0, 0)),
        at((1, 8, 128), (24, 0, 0)),
        at((1, 1, 256), (24, 0, 0)),
        at((1, 1, 256), (24, 0, 0)),
    ]
    one, coef, *faces = section(
        1,
        (fields, *halo, velocity, *halo),
        [BRICK, *FACES, whole((3, 8, 32, 128)), *own_halo],
        [brick, sds((6, 8, 32, 128), F32), *face_shapes(24)],
        [BRICK, whole((6, 8, 32, 128)), *FACES],
    )
    two, *faces = section(
        2,
        (one, fields, *exchange(faces), coef),
        [BRICK, BRICK, *FACES, whole((6, 8, 32, 128))],
        [brick, *face_shapes(24)],
        [BRICK, *FACES],
    )
    flowed, outgoing = section(
        3,
        (two, fields, *exchange(faces), coef, routing),
        [BRICK, BRICK, *FACES, whole((6, 8, 32, 128)), whole((128, 256))],
        [brick, sds((128, 24 * 128), BF16)],
        [BRICK, SLOTS],
    )
    arrived = swap(outgoing.reshape(128, 24, 128))
    returning, heat = pl.pallas_call(
        network_kernel,
        grid_spec=pltpu.PrefetchScalarGridSpec(
            num_scalar_prefetch=1,
            grid=(OWNED // 2,),
            in_specs=[
                whole(a.shape) for a in (arrived, w1, b1, w2, b2, w3, b3, w4, b4)
            ],
            out_specs=[whole((128, 24, 128)), whole((8, 128))],
        ),
        out_shape=[sds((128, 24, 128), jnp.int16), sds((8, 128), F32)],
        compiler_params=params(40),
    )(slots, arrived, w1, b1, w2, b2, w3, b3, w4, b4)
    owner_activity = (jnp.sum(heat[0]) / (8.0 * 128.0)).reshape(1)
    back = swap(returning).reshape(128, 24 * 128)
    reacted, *faces = pl.pallas_call(
        react_kernel,
        grid=(24 // GROUP,),
        in_specs=[BRICK, SLOTS, whole((256, 128))],
        out_specs=[BRICK, *FACES],
        out_shape=[brick, *face_shapes(24)],
        compiler_params=params(24),
    )(flowed, back, table)
    updated = pl.pallas_call(
        diffuse_kernel,
        grid=(24 // GROUP,),
        in_specs=[pl.BlockSpec(memory_space=pltpu.SMEM), BRICK, *FACES],
        out_specs=BRICK,
        out_shape=brick,
        scratch_shapes=[pltpu.VMEM((GROUP, 256, 128), F32)],
        compiler_params=params(24),
    )(diffusivity, reacted, *exchange(faces))
    return (updated, owner_activity)


def solution(mesh):
    return jax.shard_map(
        local,
        mesh=mesh,
        in_specs=(
            P(None, *ALL),
            P(None, *ALL),
            *(P(),) * 9,
            P(ALL, None),
            P(ALL, None),
        ),
        out_specs=(P(None, *ALL), P(ALL)),
        check_vma=False,
    )
```

```python
import functools

import jax
import jax.numpy as jnp
from jax import lax
from jax.experimental import pallas as pl
from jax.experimental.pallas import tpu as pltpu
from jax.sharding import PartitionSpec as P

GROUP = 4
TOGETHER = 8
LISTED = 96
ALL = ("gx", "gy", "gz")
F32, BF16 = jnp.float32, jnp.bfloat16
TN = (((0,), (0,)), ((), ()))
NT = (((1,), (1,)), ((), ()))


def one_hot_ends():
    rows = lax.broadcasted_iota(jnp.int32, (16, 128), 0)
    lanes = lax.broadcasted_iota(jnp.int32, (16, 128), 1)
    return (((rows == 0) & (lanes == 0)) | ((rows == 1) & (lanes == 127))).astype(F32).astype(BF16)


def z_columns(low, high):
    rows = lax.broadcasted_iota(jnp.int32, (16, 256), 0)
    pair = jnp.where(rows == 0, low, jnp.where(rows == 1, high, 0.0)).astype(BF16)
    return lax.dot_general(pair, one_hot_ends(), TN, preferred_element_type=F32)


def z_ends(cells):
    return lax.dot_general(one_hot_ends(), cells.astype(BF16), NT, preferred_element_type=F32)


def shifted(centre, y_low, y_high, z_col):
    rows = lax.broadcasted_iota(jnp.int32, (32, 128), 0)
    lanes = lax.broadcasted_iota(jnp.int32, (32, 128), 1)
    y_next = jnp.where(rows == 31, y_high, pltpu.roll(centre, 31, 0))
    y_prev = jnp.where(rows == 0, y_low, pltpu.roll(centre, 1, 0))
    z_next = jnp.where(lanes == 127, z_col, pltpu.roll(centre, 127, 1))
    z_prev = jnp.where(lanes == 0, z_col, pltpu.roll(centre, 1, 1))
    return y_next, y_prev, z_next, z_prev


def put_faces(new, f, x, xf, xl, yf, yl):
    if x == 0:
        xf[f] = new.astype(BF16)
    if x == 7:
        xl[f] = new.astype(BF16)
    yf[f, x : x + 1] = new[0:1]
    yl[f, x : x + 1] = new[31:32]


def put_z_faces(out, f, zf, zl):
    ends = z_ends(out[f].reshape(256, 128))
    zf[f] = ends[0:1]
    zl[f] = ends[1:2]


def prep_kernel(fields, velocity, xf, xl, yf, yl, zf, zl):
    def put(ref, i, f):
        xf[f] = ref[i, 0].astype(BF16)
        xl[f] = ref[i, 7].astype(BF16)
        for x in range(8):
            yf[f, x : x + 1] = ref[i, x, 0:1]
            yl[f, x : x + 1] = ref[i, x, 31:32]
        ends = z_ends(ref[i].reshape(256, 128))
        zf[f] = ends[0:1]
        zl[f] = ends[1:2]

    for f in range(24):
        put(fields, f, f)
    xf[24] = velocity[0, 0].astype(BF16)
    xl[24] = velocity[0, 7].astype(BF16)
    for x in range(8):
        yf[24, x : x + 1] = velocity[1, x, 0:1]
        yl[24, x : x + 1] = velocity[1, x, 31:32]
    ends = z_ends(velocity[2].reshape(256, 128))
    zf[24] = ends[0:1]
    zl[24] = ends[1:2]


def section_kernel(kind, *refs):
    refs = list(refs)
    q = refs.pop(0)
    start = q if kind == 1 else refs.pop(0)
    xlo, xhi, ylo, yhi, zlo, zhi = refs[:6]
    del refs[:6]
    if kind == 1:
        velocity, vxlo, vxhi, vylo, vyhi, vzlo, vzhi = refs[:7]
        del refs[:7]
    else:
        coef = refs.pop(0)
    out = refs.pop(0)
    if kind == 1:
        coef = refs.pop(0)
    if kind < 3:
        xf, xl, yf, yl, zf, zl = refs[:6]
        del refs[:6]
    zcol = refs.pop(0)

    if kind == 1:

        @pl.when(pl.program_id(0) == 0)
        def _():
            zcol[0] = z_columns(vzlo[0], vzhi[0])
            for x in range(8):
                before = vxlo[0].astype(F32) if x == 0 else velocity[0, x - 1]
                after = vxhi[0].astype(F32) if x == 7 else velocity[0, x + 1]
                y_next, y_prev, _, _ = shifted(
                    velocity[1, x], vylo[0, x : x + 1], vyhi[0, x : x + 1], velocity[1, x]
                )
                _, _, z_next, z_prev = shifted(
                    velocity[2, x], vylo[0, x : x + 1], vyhi[0, x : x + 1], zcol[0, 32 * x : 32 * x + 32]
                )
                coef[0, x] = 0.05 - 0.5 * after
                coef[1, x] = 0.05 + 0.5 * before
                coef[2, x] = 0.05 - 0.5 * y_next
                coef[3, x] = 0.05 + 0.5 * y_prev
                coef[4, x] = 0.05 - 0.5 * z_next
                coef[5, x] = 0.05 + 0.5 * z_prev

    for f in range(GROUP):
        zcol[f] = z_columns(zlo[f], zhi[f])
    for x in range(8):
        ce = [coef[i, x] for i in range(6)]
        for f in range(GROUP):
            centre = q[f, x]
            before = xlo[f].astype(F32) if x == 0 else q[f, x - 1]
            after = xhi[f].astype(F32) if x == 7 else q[f, x + 1]
            y_next, y_prev, z_next, z_prev = shifted(
                centre, ylo[f, x : x + 1], yhi[f, x : x + 1], zcol[f, 32 * x : 32 * x + 32]
            )
            moved = (
                0.7 * centre
                + (ce[0] * after + ce[1] * before)
                + (ce[2] * y_next + ce[3] * y_prev)
                + (ce[4] * z_next + ce[5] * z_prev)
            )
            if kind == 1:
                new = moved
            elif kind == 2:
                new = 0.75 * start[f, x] + 0.25 * moved
            else:
                new = (1.0 / 3.0) * start[f, x] + (2.0 / 3.0) * moved
            out[f, x] = new
            if kind < 3:
                put_faces(new, f, x, xf, xl, yf, yl)
    if kind < 3:
        for f in range(GROUP):
            put_z_faces(out, f, zf, zl)


def diffuse_kernel(rates, q, xlo, xhi, ylo, yhi, zlo, zhi, out, zcol):
    base = pl.program_id(0) * GROUP
    for f in range(GROUP):
        zcol[f] = z_columns(zlo[f], zhi[f])
        rate = rates[base + f]
        for x in range(8):
            centre = q[f, x]
            before = xlo[f].astype(F32) if x == 0 else q[f, x - 1]
            after = xhi[f].astype(F32) if x == 7 else q[f, x + 1]
            y_next, y_prev, z_next, z_prev = shifted(
                centre, ylo[f, x : x + 1], yhi[f, x : x + 1], zcol[f, 32 * x : 32 * x + 32]
            )
            spread = (after + before) + (y_next + y_prev) + (z_next + z_prev) - 6.0 * centre
            out[f, x] = centre + rate * spread


def network_kernel(listed, flowed, w1, b1, w2, b2, w3, b3, w4, b4, out, heat, xf, xl, yf, yl, zf, zl):
    def copy(f, carry):
        rows = pl.ds(pl.multiple_of(256 * f, 256), 256)
        out[rows, :] = flowed[rows, :]
        return carry

    def activated(weights, bias, cells):
        half = jnp.dot(weights[...], cells, preferred_element_type=F32)
        half = half + jnp.concatenate([bias[...]] * TOGETHER, axis=1)
        return (half + half * jnp.tanh(half)).astype(BF16)

    def react(step, carry):
        first = step * TOGETHER
        rows = [pl.ds(listed[1 + first + j], 24, stride=256) for j in range(TOGETHER)]
        before = [flowed[r, :] for r in rows]
        hidden = activated(w1, b1, jnp.concatenate(before, axis=1).astype(BF16))
        hidden = activated(w2, b2, hidden)
        hidden = activated(w3, b3, hidden)
        result = jnp.dot(w4[...], hidden, preferred_element_type=F32)
        result = result + jnp.concatenate([b4[...]] * TOGETHER, axis=1)
        for j in range(TOGETHER):
            increment = result[:, 128 * j : 128 * j + 128]
            out[rows[j], :] = before[j] + increment
            heat[pl.ds(first + j, 1), :] = increment[0:1] * increment[0:1]
        return carry

    def faces(f, carry):
        base = pl.multiple_of(256 * f, 256)
        xf[f] = out[pl.ds(base, 32), :].astype(BF16)
        xl[f] = out[pl.ds(base + 224, 32), :].astype(BF16)
        yf[f] = out[pl.ds(base, 8, stride=32), :]
        yl[f] = out[pl.ds(base + 31, 8, stride=32), :]
        ends = z_ends(out[pl.ds(base, 256), :])
        zf[f] = ends[0:1]
        zl[f] = ends[1:2]
        return carry

    lax.fori_loop(0, 24, copy, 0)
    lax.fori_loop(0, (listed[0] + TOGETHER - 1) // TOGETHER, react, 0)
    lax.fori_loop(0, 24, faces, 0)


def params(mib):
    return pltpu.CompilerParams(vmem_limit_bytes=mib * 1024 * 1024)


def sds(shape, dtype):
    return jax.ShapeDtypeStruct(shape, dtype)


def whole(shape):
    return pl.BlockSpec(shape, lambda *_: (0,) * len(shape))


def at(shape, place):
    return pl.BlockSpec(shape, lambda *_: place)


BRICK = pl.BlockSpec((GROUP, 8, 32, 128), lambda g, *_: (g, 0, 0, 0))
X_FACE = pl.BlockSpec((GROUP, 32, 128), lambda g, *_: (g, 0, 0))
Y_FACE = pl.BlockSpec((GROUP, 8, 128), lambda g, *_: (g, 0, 0))
Z_FACE = pl.BlockSpec((GROUP, 1, 256), lambda g, *_: (g, 0, 0))
FACES = [X_FACE, X_FACE, Y_FACE, Y_FACE, Z_FACE, Z_FACE]


def face_shapes(count):
    return [
        sds((count, 32, 128), BF16),
        sds((count, 32, 128), BF16),
        sds((count, 8, 128), F32),
        sds((count, 8, 128), F32),
        sds((count, 1, 256), F32),
        sds((count, 1, 256), F32),
    ]


def exchange(faces):
    got = []
    for axis, first, last in zip(ALL, faces[0::2], faces[1::2]):
        n = lax.axis_size(axis)
        got.append(lax.ppermute(last, axis, [(i, (i + 1) % n) for i in range(n)]))
        got.append(lax.ppermute(first, axis, [((i + 1) % n, i) for i in range(n)]))
    return got


def section(kind, args, in_specs, out_shapes, out_specs):
    return pl.pallas_call(
        functools.partial(section_kernel, kind),
        grid=(24 // GROUP,),
        in_specs=in_specs,
        out_specs=out_specs,
        out_shape=out_shapes,
        scratch_shapes=[pltpu.VMEM((GROUP, 256, 128), F32)],
        compiler_params=params(24),
    )(*args)


def swap(tiles):
    return lax.all_to_all(tiles, ALL, split_axis=0, concat_axis=0, tiled=True)


def local(
    fields,
    velocity,
    diffusivity,
    weight_in,
    bias_in,
    weight_mid,
    bias_mid,
    weight_low,
    bias_low,
    weight_out,
    bias_out,
    react_list,
    owner_table,
):
    brick = sds(fields.shape, F32)
    ids, owners = react_list[0], owner_table[0]
    count = jnp.sum((ids >= 0).astype(jnp.int32))
    listed = jnp.concatenate([count[None], jnp.where(ids >= 0, ids, ids[0])])
    half = jnp.asarray(0.5, BF16)
    w1, w2, w3, w4 = (weight_in * half).T, (weight_mid * half).T, (weight_low * half).T, weight_out.T
    b1, b2, b3, b4 = (
        jnp.broadcast_to((s * b)[:, None], (b.shape[0], 128))
        for s, b in ((0.5, bias_in), (0.5, bias_mid), (0.5, bias_low), (1.0, bias_out))
    )

    faces = pl.pallas_call(
        prep_kernel, out_shape=face_shapes(25), compiler_params=params(24)
    )(fields, velocity)
    halo = exchange(faces)
    own_halo = [
        at((1, 32, 128), (24, 0, 0)),
        at((1, 32, 128), (24, 0, 0)),
        at((1, 8, 128), (24, 0, 0)),
        at((1, 8, 128), (24, 0, 0)),
        at((1, 1, 256), (24, 0, 0)),
        at((1, 1, 256), (24, 0, 0)),
    ]
    one, coef, *faces = section(
        1,
        (fields, *halo, velocity, *halo),
        [BRICK, *FACES, whole((3, 8, 32, 128)), *own_halo],
        [brick, sds((6, 8, 32, 128), F32), *face_shapes(24)],
        [BRICK, whole((6, 8, 32, 128)), *FACES],
    )
    two, *faces = section(
        2,
        (one, fields, *exchange(faces), coef),
        [BRICK, BRICK, *FACES, whole((6, 8, 32, 128))],
        [brick, *face_shapes(24)],
        [BRICK, *FACES],
    )
    (flowed,) = section(
        3,
        (two, fields, *exchange(faces), coef),
        [BRICK, BRICK, *FACES, whole((6, 8, 32, 128))],
        [brick],
        [BRICK],
    )
    in_vmem = pl.BlockSpec(memory_space=pltpu.VMEM)
    reacted, heat, *faces = pl.pallas_call(
        network_kernel,
        in_specs=[pl.BlockSpec(memory_space=pltpu.SMEM)] + [in_vmem] * 9,
        out_specs=[in_vmem] * 8,
        out_shape=[sds((24 * 256, 128), F32), sds((LISTED, 128), F32), *face_shapes(24)],
        compiler_params=params(56),
    )(listed, flowed.reshape(24 * 256, 128), w1, b1, w2, b2, w3, b3, w4, b4)
    reacted = reacted.reshape(fields.shape)
    mean_heat = jnp.mean(heat, axis=1)
    owned_by = owners[None, :] == jnp.arange(128, dtype=jnp.int32)[:, None]
    by_owner = jnp.sum(jnp.where(owned_by, mean_heat[None, :], 0.0), axis=1)
    around = exchange(faces)
    sent = jnp.broadcast_to(by_owner[:, None, None], (128, 1, 128))
    owner_activity = (jnp.sum(swap(sent)[:, 0, 0]) / 8.0).reshape(1)
    updated = pl.pallas_call(
        diffuse_kernel,
        grid=(24 // GROUP,),
        in_specs=[pl.BlockSpec(memory_space=pltpu.SMEM), BRICK, *FACES],
        out_specs=BRICK,
        out_shape=brick,
        scratch_shapes=[pltpu.VMEM((GROUP, 256, 128), F32)],
        compiler_params=params(24),
    )(diffusivity, reacted, *around)
    return (updated, owner_activity)


def solution(mesh):
    return jax.shard_map(
        local,
        mesh=mesh,
        in_specs=(
            P(None, *ALL),
            P(None, *ALL),
            *(P(),) * 9,
            P(ALL, None),
            P(ALL, None),
        ),
        out_specs=(P(None, *ALL), P(ALL)),
        check_vma=False,
    )
```

```python
import functools

import jax
import jax.numpy as jnp
from jax import lax
from jax.experimental import pallas as pl
from jax.experimental.pallas import tpu as pltpu
from jax.sharding import PartitionSpec as P

GROUP = 4
TOGETHER = 8
LISTED = 96
NETWORK_MIB = 30
ALL = ("gx", "gy", "gz")
F32, BF16 = jnp.float32, jnp.bfloat16
TN = (((0,), (0,)), ((), ()))
NT = (((1,), (1,)), ((), ()))


def one_hot_ends():
    rows = lax.broadcasted_iota(jnp.int32, (16, 128), 0)
    lanes = lax.broadcasted_iota(jnp.int32, (16, 128), 1)
    return (((rows == 0) & (lanes == 0)) | ((rows == 1) & (lanes == 127))).astype(F32).astype(BF16)


def z_columns(low, high):
    rows = lax.broadcasted_iota(jnp.int32, (16, 256), 0)
    pair = jnp.where(rows == 0, low, jnp.where(rows == 1, high, 0.0)).astype(BF16)
    return lax.dot_general(pair, one_hot_ends(), TN, preferred_element_type=F32)


def z_ends(cells):
    return lax.dot_general(one_hot_ends(), cells.astype(BF16), NT, preferred_element_type=F32)


def shifted(centre, y_low, y_high, z_col):
    rows = lax.broadcasted_iota(jnp.int32, (32, 128), 0)
    lanes = lax.broadcasted_iota(jnp.int32, (32, 128), 1)
    y_next = jnp.where(rows == 31, y_high, pltpu.roll(centre, 31, 0))
    y_prev = jnp.where(rows == 0, y_low, pltpu.roll(centre, 1, 0))
    z_next = jnp.where(lanes == 127, z_col, pltpu.roll(centre, 127, 1))
    z_prev = jnp.where(lanes == 0, z_col, pltpu.roll(centre, 1, 1))
    return y_next, y_prev, z_next, z_prev


def put_faces(new, f, x, xf, xl, yf, yl):
    if x == 0:
        xf[f] = new.astype(BF16)
    if x == 7:
        xl[f] = new.astype(BF16)
    yf[f, x : x + 1] = new[0:1]
    yl[f, x : x + 1] = new[31:32]


def put_z_faces(out, f, zf, zl):
    ends = z_ends(out[f].reshape(256, 128))
    zf[f] = ends[0:1]
    zl[f] = ends[1:2]


def prep_kernel(fields, velocity, xf, xl, yf, yl, zf, zl):
    def put(ref, i, f):
        xf[f] = ref[i, 0].astype(BF16)
        xl[f] = ref[i, 7].astype(BF16)
        for x in range(8):
            yf[f, x : x + 1] = ref[i, x, 0:1]
            yl[f, x : x + 1] = ref[i, x, 31:32]
        ends = z_ends(ref[i].reshape(256, 128))
        zf[f] = ends[0:1]
        zl[f] = ends[1:2]

    for f in range(24):
        put(fields, f, f)
    xf[24] = velocity[0, 0].astype(BF16)
    xl[24] = velocity[0, 7].astype(BF16)
    for x in range(8):
        yf[24, x : x + 1] = velocity[1, x, 0:1]
        yl[24, x : x + 1] = velocity[1, x, 31:32]
    ends = z_ends(velocity[2].reshape(256, 128))
    zf[24] = ends[0:1]
    zl[24] = ends[1:2]


def section_kernel(kind, *refs):
    refs = list(refs)
    q = refs.pop(0)
    start = q if kind == 1 else refs.pop(0)
    xlo, xhi, ylo, yhi, zlo, zhi = refs[:6]
    del refs[:6]
    if kind == 1:
        velocity, vxlo, vxhi, vylo, vyhi, vzlo, vzhi = refs[:7]
        del refs[:7]
    else:
        coef = refs.pop(0)
    out = refs.pop(0)
    if kind == 1:
        coef = refs.pop(0)
    if kind < 3:
        xf, xl, yf, yl, zf, zl = refs[:6]
        del refs[:6]
    zcol = refs.pop(0)

    if kind == 1:

        @pl.when(pl.program_id(0) == 0)
        def _():
            zcol[0] = z_columns(vzlo[0], vzhi[0])
            for x in range(8):
                before = vxlo[0].astype(F32) if x == 0 else velocity[0, x - 1]
                after = vxhi[0].astype(F32) if x == 7 else velocity[0, x + 1]
                y_next, y_prev, _, _ = shifted(
                    velocity[1, x], vylo[0, x : x + 1], vyhi[0, x : x + 1], velocity[1, x]
                )
                _, _, z_next, z_prev = shifted(
                    velocity[2, x], vylo[0, x : x + 1], vyhi[0, x : x + 1], zcol[0, 32 * x : 32 * x + 32]
                )
                coef[0, x] = 0.05 - 0.5 * after
                coef[1, x] = 0.05 + 0.5 * before
                coef[2, x] = 0.05 - 0.5 * y_next
                coef[3, x] = 0.05 + 0.5 * y_prev
                coef[4, x] = 0.05 - 0.5 * z_next
                coef[5, x] = 0.05 + 0.5 * z_prev

    for f in range(GROUP):
        zcol[f] = z_columns(zlo[f], zhi[f])
    for x in range(8):
        ce = [coef[i, x] for i in range(6)]
        for f in range(GROUP):
            centre = q[f, x]
            before = xlo[f].astype(F32) if x == 0 else q[f, x - 1]
            after = xhi[f].astype(F32) if x == 7 else q[f, x + 1]
            y_next, y_prev, z_next, z_prev = shifted(
                centre, ylo[f, x : x + 1], yhi[f, x : x + 1], zcol[f, 32 * x : 32 * x + 32]
            )
            moved = (
                0.7 * centre
                + (ce[0] * after + ce[1] * before)
                + (ce[2] * y_next + ce[3] * y_prev)
                + (ce[4] * z_next + ce[5] * z_prev)
            )
            if kind == 1:
                new = moved
            elif kind == 2:
                new = 0.75 * start[f, x] + 0.25 * moved
            else:
                new = (1.0 / 3.0) * start[f, x] + (2.0 / 3.0) * moved
            out[f, x] = new
            if kind < 3:
                put_faces(new, f, x, xf, xl, yf, yl)
    if kind < 3:
        for f in range(GROUP):
            put_z_faces(out, f, zf, zl)


def diffuse_kernel(rates, q, xlo, xhi, ylo, yhi, zlo, zhi, out, zcol):
    base = pl.program_id(0) * GROUP
    for f in range(GROUP):
        zcol[f] = z_columns(zlo[f], zhi[f])
        rate = rates[base + f]
        for x in range(8):
            centre = q[f, x]
            before = xlo[f].astype(F32) if x == 0 else q[f, x - 1]
            after = xhi[f].astype(F32) if x == 7 else q[f, x + 1]
            y_next, y_prev, z_next, z_prev = shifted(
                centre, ylo[f, x : x + 1], yhi[f, x : x + 1], zcol[f, 32 * x : 32 * x + 32]
            )
            spread = (after + before) + (y_next + y_prev) + (z_next + z_prev) - 6.0 * centre
            out[f, x] = centre + rate * spread


def columns_kernel(weights, *refs):
    refs[4][...] = weights[...].astype(F32).T.astype(BF16)
    for row, out in zip(refs[:4], refs[5:]):
        out[...] = jnp.broadcast_to(row[...], (128, row.shape[1])).T


def network_kernel(listed, flowed, owned_by, w1, b1, b2, b3, b4, w2, w3, w4, out, sent, xf, xl, yf, yl, zf, zl, heat):
    def copy(f, carry):
        rows = pl.ds(pl.multiple_of(256 * f, 256), 256)
        out[rows, :] = flowed[rows, :]
        return carry

    def activated(weights, bias, cells):
        half = jnp.dot(weights[...], cells, preferred_element_type=F32)
        half = 0.5 * (half + jnp.concatenate([bias[...]] * TOGETHER, axis=1))
        return (half + half * jnp.tanh(half)).astype(BF16)

    def react(step, carry):
        first = step * TOGETHER
        rows = [pl.ds(listed[1 + first + j], 24, stride=256) for j in range(TOGETHER)]
        before = [flowed[r, :] for r in rows]
        hidden = activated(w1, b1, jnp.concatenate(before, axis=1).astype(BF16))
        hidden = activated(w2, b2, hidden)
        hidden = activated(w3, b3, hidden)
        result = jnp.dot(w4[...], hidden, preferred_element_type=F32)
        result = result + jnp.concatenate([b4[...]] * TOGETHER, axis=1)
        for j in range(TOGETHER):
            increment = result[:, 128 * j : 128 * j + 128]
            out[rows[j], :] = before[j] + increment
            heat[pl.ds(first + j, 1), :] = increment[0:1] * increment[0:1]
        return carry

    def faces(f, carry):
        base = pl.multiple_of(256 * f, 256)
        xf[f] = out[pl.ds(base, 32), :].astype(BF16)
        xl[f] = out[pl.ds(base + 224, 32), :].astype(BF16)
        yf[f] = out[pl.ds(base, 8, stride=32), :]
        yl[f] = out[pl.ds(base + 31, 8, stride=32), :]
        ends = z_ends(out[pl.ds(base, 256), :])
        zf[f] = ends[0:1]
        zl[f] = ends[1:2]
        return carry

    heat[...] = jnp.zeros_like(heat)
    lax.fori_loop(0, 24, copy, 0)
    lax.fori_loop(0, (listed[0] + TOGETHER - 1) // TOGETHER, react, 0)
    lax.fori_loop(0, 24, faces, 0)
    sent[...] = jnp.dot(
        owned_by[...], heat[...], preferred_element_type=F32, precision=lax.Precision.HIGHEST
    )


def params(mib):
    return pltpu.CompilerParams(vmem_limit_bytes=mib * 1024 * 1024)


def sds(shape, dtype):
    return jax.ShapeDtypeStruct(shape, dtype)


def whole(shape):
    return pl.BlockSpec(shape, lambda *_: (0,) * len(shape))


def at(shape, place):
    return pl.BlockSpec(shape, lambda *_: place)


BRICK = pl.BlockSpec((GROUP, 8, 32, 128), lambda g, *_: (g, 0, 0, 0))
X_FACE = pl.BlockSpec((GROUP, 32, 128), lambda g, *_: (g, 0, 0))
Y_FACE = pl.BlockSpec((GROUP, 8, 128), lambda g, *_: (g, 0, 0))
Z_FACE = pl.BlockSpec((GROUP, 1, 256), lambda g, *_: (g, 0, 0))
FACES = [X_FACE, X_FACE, Y_FACE, Y_FACE, Z_FACE, Z_FACE]


def face_shapes(count):
    return [
        sds((count, 32, 128), BF16),
        sds((count, 32, 128), BF16),
        sds((count, 8, 128), F32),
        sds((count, 8, 128), F32),
        sds((count, 1, 256), F32),
        sds((count, 1, 256), F32),
    ]


def exchange(faces):
    got = []
    for axis, first, last in zip(ALL, faces[0::2], faces[1::2]):
        n = lax.axis_size(axis)
        got.append(lax.ppermute(last, axis, [(i, (i + 1) % n) for i in range(n)]))
        got.append(lax.ppermute(first, axis, [((i + 1) % n, i) for i in range(n)]))
    return got


def section(kind, args, in_specs, out_shapes, out_specs):
    return pl.pallas_call(
        functools.partial(section_kernel, kind),
        grid=(24 // GROUP,),
        in_specs=in_specs,
        out_specs=out_specs,
        out_shape=out_shapes,
        scratch_shapes=[pltpu.VMEM((GROUP, 256, 128), F32)],
        compiler_params=params(24),
    )(*args)


def swap(tiles):
    return lax.all_to_all(tiles, ALL, split_axis=0, concat_axis=0, tiled=True)


def local(
    fields,
    velocity,
    diffusivity,
    weight_in,
    bias_in,
    weight_mid,
    bias_mid,
    weight_low,
    bias_low,
    weight_out,
    bias_out,
    react_list,
    owner_table,
):
    brick = sds(fields.shape, F32)
    ids, owners = react_list[0], owner_table[0]
    count = jnp.sum((ids >= 0).astype(jnp.int32))
    listed = jnp.concatenate([count[None], jnp.where(ids >= 0, ids, ids[0])])
    owned_by = (owners[None, :] == jnp.arange(128, dtype=jnp.int32)[:, None]).astype(F32)

    faces = pl.pallas_call(
        prep_kernel, out_shape=face_shapes(25), compiler_params=params(24)
    )(fields, velocity)
    halo = exchange(faces)
    own_halo = [
        at((1, 32, 128), (24, 0, 0)),
        at((1, 32, 128), (24, 0, 0)),
        at((1, 8, 128), (24, 0, 0)),
        at((1, 8, 128), (24, 0, 0)),
        at((1, 1, 256), (24, 0, 0)),
        at((1, 1, 256), (24, 0, 0)),
    ]
    one, coef, *faces = section(
        1,
        (fields, *halo, velocity, *halo),
        [BRICK, *FACES, whole((3, 8, 32, 128)), *own_halo],
        [brick, sds((6, 8, 32, 128), F32), *face_shapes(24)],
        [BRICK, whole((6, 8, 32, 128)), *FACES],
    )
    biases = (bias_in, bias_mid, bias_low, bias_out)
    one, *given = lax.optimization_barrier((one, weight_in, *(b.reshape(1, -1) for b in biases)))
    columns = pl.pallas_call(
        columns_kernel,
        out_shape=[sds(weight_in.shape[::-1], BF16), *(sds((b.shape[0], 128), F32) for b in biases)],
        compiler_params=params(16),
        cost_estimate=pl.CostEstimate(flops=0, bytes_accessed=4 * 2**20, transcendentals=0),
    )(*given)
    two, *faces = section(
        2,
        (one, fields, *exchange(faces), coef),
        [BRICK, BRICK, *FACES, whole((6, 8, 32, 128))],
        [brick, *face_shapes(24)],
        [BRICK, *FACES],
    )
    (flowed,) = section(
        3,
        (two, fields, *exchange(faces), coef),
        [BRICK, BRICK, *FACES, whole((6, 8, 32, 128))],
        [brick],
        [BRICK],
    )
    in_vmem = pl.BlockSpec(memory_space=pltpu.VMEM)
    reacted, sent, *faces = pl.pallas_call(
        network_kernel,
        in_specs=[pl.BlockSpec(memory_space=pltpu.SMEM)] + [in_vmem] * 10,
        out_specs=[in_vmem] * 8,
        out_shape=[sds((24 * 256, 128), F32), sds((128, 128), F32), *face_shapes(24)],
        scratch_shapes=[pltpu.VMEM((LISTED, 128), F32)],
        compiler_params=params(NETWORK_MIB),
    )(listed, flowed.reshape(24 * 256, 128), owned_by, *columns, weight_mid.T, weight_low.T, weight_out.T)
    reacted = reacted.reshape(fields.shape)
    around = exchange(faces)
    heats = swap(sent.reshape(128, 1, 128))
    updated = pl.pallas_call(
        diffuse_kernel,
        grid=(24 // GROUP,),
        in_specs=[pl.BlockSpec(memory_space=pltpu.SMEM), BRICK, *FACES],
        out_specs=BRICK,
        out_shape=brick,
        scratch_shapes=[pltpu.VMEM((GROUP, 256, 128), F32)],
        compiler_params=params(24),
        cost_estimate=pl.CostEstimate(flops=10**9, bytes_accessed=24 * 2**20, transcendentals=0),
    )(diffusivity, reacted, *around)
    heats, updated = lax.optimization_barrier((heats, updated))
    owner_activity = (jnp.sum(heats) / (8.0 * 128.0)).reshape(1)
    return (updated, owner_activity)


def solution(mesh):
    return jax.shard_map(
        local,
        mesh=mesh,
        in_specs=(
            P(None, *ALL),
            P(None, *ALL),
            *(P(),) * 9,
            P(ALL, None),
            P(ALL, None),
        ),
        out_specs=(P(None, *ALL), P(ALL)),
        check_vma=False,
    )
```

```python
import functools

import jax
import jax.numpy as jnp
from jax import lax
from jax.experimental import pallas as pl
from jax.experimental.pallas import tpu as pltpu
from jax.sharding import PartitionSpec as P

GROUP = 12
TOGETHER = 12
SPREAD = 8
LISTED = 96
NETWORK_MIB = 38
ALL = ("gx", "gy", "gz")
F32, BF16 = jnp.float32, jnp.bfloat16
TN = (((0,), (0,)), ((), ()))
NT = (((1,), (1,)), ((), ()))


def one_hot_ends():
    rows = lax.broadcasted_iota(jnp.int32, (16, 128), 0)
    lanes = lax.broadcasted_iota(jnp.int32, (16, 128), 1)
    return (((rows == 0) & (lanes == 0)) | ((rows == 1) & (lanes == 127))).astype(F32).astype(BF16)


def z_columns(low, high):
    rows = lax.broadcasted_iota(jnp.int32, (16, 256), 0)
    pair = jnp.where(rows == 0, low, jnp.where(rows == 1, high, 0.0)).astype(BF16)
    return lax.dot_general(pair, one_hot_ends(), TN, preferred_element_type=F32)


def z_ends(cells):
    return lax.dot_general(one_hot_ends(), cells.astype(BF16), NT, preferred_element_type=F32)


def shifted(centre, y_low, y_high, z_col):
    rows = lax.broadcasted_iota(jnp.int32, (32, 128), 0)
    lanes = lax.broadcasted_iota(jnp.int32, (32, 128), 1)
    y_next = jnp.where(rows == 31, y_high, pltpu.roll(centre, 31, 0))
    y_prev = jnp.where(rows == 0, y_low, pltpu.roll(centre, 1, 0))
    z_next = jnp.where(lanes == 127, z_col, pltpu.roll(centre, 127, 1))
    z_prev = jnp.where(lanes == 0, z_col, pltpu.roll(centre, 1, 1))
    return y_next, y_prev, z_next, z_prev


def put_faces(new, f, x, xf, xl, yf, yl):
    if x == 0:
        xf[f] = new.astype(BF16)
    if x == 7:
        xl[f] = new.astype(BF16)
    yf[f, x : x + 1] = new[0:1]
    yl[f, x : x + 1] = new[31:32]


def put_z_faces(out, f, zf, zl):
    ends = z_ends(out[f].reshape(256, 128))
    zf[f] = ends[0:1]
    zl[f] = ends[1:2]


def prep_kernel(fields, velocity, xf, xl, yf, yl, zf, zl):
    def put(ref, i, f):
        xf[f] = ref[i, 0].astype(BF16)
        xl[f] = ref[i, 7].astype(BF16)
        for x in range(8):
            yf[f, x : x + 1] = ref[i, x, 0:1]
            yl[f, x : x + 1] = ref[i, x, 31:32]
        ends = z_ends(ref[i].reshape(256, 128))
        zf[f] = ends[0:1]
        zl[f] = ends[1:2]

    for f in range(24):
        put(fields, f, f)
    xf[24] = velocity[0, 0].astype(BF16)
    xl[24] = velocity[0, 7].astype(BF16)
    for x in range(8):
        yf[24, x : x + 1] = velocity[1, x, 0:1]
        yl[24, x : x + 1] = velocity[1, x, 31:32]
    ends = z_ends(velocity[2].reshape(256, 128))
    zf[24] = ends[0:1]
    zl[24] = ends[1:2]


def section_kernel(kind, *refs):
    refs = list(refs)
    q = refs.pop(0)
    start = q if kind == 1 else refs.pop(0)
    xlo, xhi, ylo, yhi, zlo, zhi = refs[:6]
    del refs[:6]
    if kind == 1:
        velocity, vxlo, vxhi, vylo, vyhi, vzlo, vzhi = refs[:7]
        del refs[:7]
    else:
        coef = refs.pop(0)
    out = refs.pop(0)
    if kind == 1:
        coef = refs.pop(0)
    if kind < 3:
        xf, xl, yf, yl, zf, zl = refs[:6]
        del refs[:6]
    zcol = refs.pop(0)

    if kind == 1:

        @pl.when(pl.program_id(0) == 0)
        def _():
            zcol[0] = z_columns(vzlo[0], vzhi[0])
            for x in range(8):
                before = vxlo[0].astype(F32) if x == 0 else velocity[0, x - 1]
                after = vxhi[0].astype(F32) if x == 7 else velocity[0, x + 1]
                y_next, y_prev, _, _ = shifted(
                    velocity[1, x], vylo[0, x : x + 1], vyhi[0, x : x + 1], velocity[1, x]
                )
                _, _, z_next, z_prev = shifted(
                    velocity[2, x], vylo[0, x : x + 1], vyhi[0, x : x + 1], zcol[0, 32 * x : 32 * x + 32]
                )
                coef[0, x] = 0.05 - 0.5 * after
                coef[1, x] = 0.05 + 0.5 * before
                coef[2, x] = 0.05 - 0.5 * y_next
                coef[3, x] = 0.05 + 0.5 * y_prev
                coef[4, x] = 0.05 - 0.5 * z_next
                coef[5, x] = 0.05 + 0.5 * z_prev

    for f in range(GROUP):
        zcol[f] = z_columns(zlo[f], zhi[f])
    for x in range(8):
        ce = [coef[i, x] for i in range(6)]
        for f in range(GROUP):
            centre = q[f, x]
            before = xlo[f].astype(F32) if x == 0 else q[f, x - 1]
            after = xhi[f].astype(F32) if x == 7 else q[f, x + 1]
            y_next, y_prev, z_next, z_prev = shifted(
                centre, ylo[f, x : x + 1], yhi[f, x : x + 1], zcol[f, 32 * x : 32 * x + 32]
            )
            moved = (
                0.7 * centre
                + (ce[0] * after + ce[1] * before)
                + (ce[2] * y_next + ce[3] * y_prev)
                + (ce[4] * z_next + ce[5] * z_prev)
            )
            if kind == 1:
                new = moved
            elif kind == 2:
                new = 0.75 * start[f, x] + 0.25 * moved
            else:
                new = (1.0 / 3.0) * start[f, x] + (2.0 / 3.0) * moved
            out[f, x] = new
            if kind < 3:
                put_faces(new, f, x, xf, xl, yf, yl)
    if kind < 3:
        for f in range(GROUP):
            put_z_faces(out, f, zf, zl)


def diffuse_kernel(rates, q, xlo, xhi, ylo, yhi, zlo, zhi, out, zcol):
    base = pl.program_id(0) * GROUP
    for f in range(GROUP):
        zcol[f] = z_columns(zlo[f], zhi[f])
        rate = rates[base + f]
        for x in range(8):
            centre = q[f, x]
            before = xlo[f].astype(F32) if x == 0 else q[f, x - 1]
            after = xhi[f].astype(F32) if x == 7 else q[f, x + 1]
            y_next, y_prev, z_next, z_prev = shifted(
                centre, ylo[f, x : x + 1], yhi[f, x : x + 1], zcol[f, 32 * x : 32 * x + 32]
            )
            spread = (after + before) + (y_next + y_prev) + (z_next + z_prev) - 6.0 * centre
            out[f, x] = centre + rate * spread


def columns_kernel(w_in, b_in, w_mid, w_low, b_mid, b_low, b_out, w1, w2, w3, b2, b3, b4):
    bias = 0.5 * b_in[...]
    parts = []
    for _ in range(3):
        parts.append(bias.astype(BF16).astype(F32))
        bias = bias - parts[-1]
    zeros = jnp.zeros((5, bias.shape[1]), F32)
    w1[...] = jnp.concatenate([0.5 * w_in[...].astype(F32), *parts, zeros], axis=0).T.astype(BF16)
    w2[...] = (0.5 * w_mid[...].astype(F32)).astype(BF16)
    w3[...] = (0.5 * w_low[...].astype(F32)).astype(BF16)
    for row, out, factor in ((b_mid, b2, 0.5), (b_low, b3, 0.5), (b_out, b4, 1.0)):
        out[...] = jnp.broadcast_to(factor * row[...], (128, row.shape[1])).T


def network_kernel(listed, flowed, owned_by, w1, w2, w3, b2, b3, b4, w4, out, sent, xf, xl, yf, yl, zf, zl, heat):
    def copy(f, carry):
        rows = pl.ds(pl.multiple_of(256 * f, 256), 256)
        out[rows, :] = flowed[rows, :]
        return carry

    def product(weights, cells):
        return jnp.dot(weights[...], cells, preferred_element_type=F32)

    def beside(bias):
        return jnp.concatenate([bias[...]] * TOGETHER, axis=1)

    def silu(half):
        return (half + half * jnp.tanh(half)).astype(BF16)

    def react(step, carry):
        first = step * TOGETHER
        rows = [pl.ds(listed[1 + first + j], 24, stride=256) for j in range(TOGETHER)]
        before = [flowed[r, :] for r in rows]
        ones = jnp.ones((8, TOGETHER * 128), F32)
        cells = jnp.concatenate([jnp.concatenate(before, axis=1), ones], axis=0).astype(BF16)
        hidden = silu(product(w1, cells))
        hidden = silu(product(w2, hidden) + beside(b2))
        hidden = silu(product(w3, hidden) + beside(b3))
        result = product(w4, hidden) + beside(b4)
        for j in range(TOGETHER):
            increment = result[:, 128 * j : 128 * j + 128]
            out[rows[j], :] = before[j] + increment
            heat[pl.ds(first + j, 1), :] = increment[0:1] * increment[0:1]
        return carry

    def faces(f, carry):
        base = pl.multiple_of(256 * f, 256)
        xf[f] = out[pl.ds(base, 32), :].astype(BF16)
        xl[f] = out[pl.ds(base + 224, 32), :].astype(BF16)
        yf[f] = out[pl.ds(base, 8, stride=32), :]
        yl[f] = out[pl.ds(base + 31, 8, stride=32), :]
        ends = z_ends(out[pl.ds(base, 256), :])
        zf[f] = ends[0:1]
        zl[f] = ends[1:2]
        return carry

    heat[...] = jnp.zeros_like(heat)
    lax.fori_loop(0, 24, copy, 0)
    lax.fori_loop(0, (listed[0] + TOGETHER - 1) // TOGETHER, react, 0)
    lax.fori_loop(0, 24, faces, 0)
    sent[...] = jnp.dot(
        owned_by[...], heat[...], preferred_element_type=F32, precision=lax.Precision.HIGHEST
    )


def params(mib):
    return pltpu.CompilerParams(vmem_limit_bytes=mib * 1024 * 1024)


def sds(shape, dtype):
    return jax.ShapeDtypeStruct(shape, dtype)


def whole(shape):
    return pl.BlockSpec(shape, lambda *_: (0,) * len(shape))


def at(shape, place):
    return pl.BlockSpec(shape, lambda *_: place)


BRICK = pl.BlockSpec((GROUP, 8, 32, 128), lambda g, *_: (g, 0, 0, 0))
X_FACE = pl.BlockSpec((GROUP, 32, 128), lambda g, *_: (g, 0, 0))
Y_FACE = pl.BlockSpec((GROUP, 8, 128), lambda g, *_: (g, 0, 0))
Z_FACE = pl.BlockSpec((GROUP, 1, 256), lambda g, *_: (g, 0, 0))
FACES = [X_FACE, X_FACE, Y_FACE, Y_FACE, Z_FACE, Z_FACE]


def face_shapes(count):
    return [
        sds((count, 32, 128), BF16),
        sds((count, 32, 128), BF16),
        sds((count, 8, 128), F32),
        sds((count, 8, 128), F32),
        sds((count, 1, 256), F32),
        sds((count, 1, 256), F32),
    ]


def exchange(faces):
    got = []
    for axis, first, last in zip(ALL, faces[0::2], faces[1::2]):
        n = lax.axis_size(axis)
        got.append(lax.ppermute(last, axis, [(i, (i + 1) % n) for i in range(n)]))
        got.append(lax.ppermute(first, axis, [((i + 1) % n, i) for i in range(n)]))
    return got


def section(kind, args, in_specs, out_shapes, out_specs):
    return pl.pallas_call(
        functools.partial(section_kernel, kind),
        grid=(24 // GROUP,),
        in_specs=in_specs,
        out_specs=out_specs,
        out_shape=out_shapes,
        scratch_shapes=[pltpu.VMEM((GROUP, 256, 128), F32)],
        compiler_params=params(32),
    )(*args)


def swap(tiles):
    return lax.all_to_all(tiles, ALL, split_axis=0, concat_axis=0, tiled=True)


def local(
    fields,
    velocity,
    diffusivity,
    weight_in,
    bias_in,
    weight_mid,
    bias_mid,
    weight_low,
    bias_low,
    weight_out,
    bias_out,
    react_list,
    owner_table,
):
    brick = sds(fields.shape, F32)
    ids, owners = react_list[0], owner_table[0]
    count = jnp.sum((ids >= 0).astype(jnp.int32))
    listed = jnp.concatenate([count[None], jnp.where(ids >= 0, ids, ids[0])])
    rows = jnp.arange(128 * SPREAD, dtype=jnp.int32)[:, None]
    owned_by = (owners[None, :] * SPREAD == rows).astype(F32)

    faces = pl.pallas_call(
        prep_kernel, out_shape=face_shapes(25), compiler_params=params(32)
    )(fields, velocity)
    halo = exchange(faces)
    own_halo = [
        at((1, 32, 128), (24, 0, 0)),
        at((1, 32, 128), (24, 0, 0)),
        at((1, 8, 128), (24, 0, 0)),
        at((1, 8, 128), (24, 0, 0)),
        at((1, 1, 256), (24, 0, 0)),
        at((1, 1, 256), (24, 0, 0)),
    ]
    one, coef, *faces = section(
        1,
        (fields, *halo, velocity, *halo),
        [BRICK, *FACES, whole((3, 8, 32, 128)), *own_halo],
        [brick, sds((6, 8, 32, 128), F32), *face_shapes(24)],
        [BRICK, whole((6, 8, 32, 128)), *FACES],
    )
    one, *given = lax.optimization_barrier(
        (
            one,
            weight_in,
            bias_in.reshape(1, -1),
            weight_mid.T,
            weight_low.T,
            *(b.reshape(1, -1) for b in (bias_mid, bias_low, bias_out)),
        )
    )
    columns = pl.pallas_call(
        columns_kernel,
        out_shape=[
            sds((weight_in.shape[1], 32), BF16),
            sds(weight_mid.shape[::-1], BF16),
            sds(weight_low.shape[::-1], BF16),
            *(sds((b.shape[0], 128), F32) for b in (bias_mid, bias_low, bias_out)),
        ],
        compiler_params=params(20),
        cost_estimate=pl.CostEstimate(flops=0, bytes_accessed=8 * 2**20, transcendentals=0),
    )(*given)
    two, *faces = section(
        2,
        (one, fields, *exchange(faces), coef),
        [BRICK, BRICK, *FACES, whole((6, 8, 32, 128))],
        [brick, *face_shapes(24)],
        [BRICK, *FACES],
    )
    (flowed,) = section(
        3,
        (two, fields, *exchange(faces), coef),
        [BRICK, BRICK, *FACES, whole((6, 8, 32, 128))],
        [brick],
        [BRICK],
    )
    in_vmem = pl.BlockSpec(memory_space=pltpu.VMEM)
    reacted, sent, *faces = pl.pallas_call(
        network_kernel,
        in_specs=[pl.BlockSpec(memory_space=pltpu.SMEM)] + [in_vmem] * 9,
        out_specs=[in_vmem] * 8,
        out_shape=[sds((24 * 256, 128), F32), sds((128 * SPREAD, 128), F32), *face_shapes(24)],
        scratch_shapes=[pltpu.VMEM((LISTED, 128), F32)],
        compiler_params=params(NETWORK_MIB),
    )(listed, flowed.reshape(24 * 256, 128), owned_by, *columns, weight_out.T)
    reacted = reacted.reshape(fields.shape)
    around = exchange(faces)
    heats = swap(sent.reshape(128, SPREAD, 128))
    updated = pl.pallas_call(
        diffuse_kernel,
        grid=(24 // GROUP,),
        in_specs=[pl.BlockSpec(memory_space=pltpu.SMEM), BRICK, *FACES],
        out_specs=BRICK,
        out_shape=brick,
        scratch_shapes=[pltpu.VMEM((GROUP, 256, 128), F32)],
        compiler_params=params(32),
        cost_estimate=pl.CostEstimate(flops=10**9, bytes_accessed=24 * 2**20, transcendentals=0),
    )(diffusivity, reacted, *around)
    heats, updated = lax.optimization_barrier((heats, updated))
    owner_activity = (jnp.sum(heats) / (8.0 * 128.0)).reshape(1)
    return (updated, owner_activity)


def solution(mesh):
    return jax.shard_map(
        local,
        mesh=mesh,
        in_specs=(
            P(None, *ALL),
            P(None, *ALL),
            *(P(),) * 9,
            P(ALL, None),
            P(ALL, None),
        ),
        out_specs=(P(None, *ALL), P(ALL)),
        check_vma=False,
    )
```

```python
import functools

import jax
import jax.numpy as jnp
from jax import lax
from jax.experimental import pallas as pl
from jax.experimental.pallas import tpu as pltpu
from jax.sharding import PartitionSpec as P

GROUP = 12
TOGETHER = 12
LISTED = 96
NETWORK_MIB = 38
ALL = ("gx", "gy", "gz")
F32, BF16 = jnp.float32, jnp.bfloat16
TN = (((0,), (0,)), ((), ()))
NT = (((1,), (1,)), ((), ()))


def one_hot_ends():
    rows = lax.broadcasted_iota(jnp.int32, (16, 128), 0)
    lanes = lax.broadcasted_iota(jnp.int32, (16, 128), 1)
    return (((rows == 0) & (lanes == 0)) | ((rows == 1) & (lanes == 127))).astype(F32).astype(BF16)


def z_columns(low, high):
    rows = lax.broadcasted_iota(jnp.int32, (16, 256), 0)
    pair = jnp.where(rows == 0, low, jnp.where(rows == 1, high, 0.0)).astype(BF16)
    return lax.dot_general(pair, one_hot_ends(), TN, preferred_element_type=F32)


def z_ends(cells):
    return lax.dot_general(one_hot_ends(), cells.astype(BF16), NT, preferred_element_type=F32)


def shifted(centre, y_low, y_high, z_col):
    rows = lax.broadcasted_iota(jnp.int32, (32, 128), 0)
    lanes = lax.broadcasted_iota(jnp.int32, (32, 128), 1)
    y_next = jnp.where(rows == 31, y_high, pltpu.roll(centre, 31, 0))
    y_prev = jnp.where(rows == 0, y_low, pltpu.roll(centre, 1, 0))
    z_next = jnp.where(lanes == 127, z_col, pltpu.roll(centre, 127, 1))
    z_prev = jnp.where(lanes == 0, z_col, pltpu.roll(centre, 1, 1))
    return y_next, y_prev, z_next, z_prev


def put_faces(new, f, x, xf, xl, yf, yl):
    if x == 0:
        xf[f] = new.astype(BF16)
    if x == 7:
        xl[f] = new.astype(BF16)
    yf[f, x : x + 1] = new[0:1]
    yl[f, x : x + 1] = new[31:32]


def put_z_faces(out, f, zf, zl):
    ends = z_ends(out[f].reshape(256, 128))
    zf[f] = ends[0:1]
    zl[f] = ends[1:2]


def prep_kernel(fields, velocity, xf, xl, yf, yl, zf, zl):
    def put(ref, i, f):
        xf[f] = ref[i, 0].astype(BF16)
        xl[f] = ref[i, 7].astype(BF16)
        for x in range(8):
            yf[f, x : x + 1] = ref[i, x, 0:1]
            yl[f, x : x + 1] = ref[i, x, 31:32]
        ends = z_ends(ref[i].reshape(256, 128))
        zf[f] = ends[0:1]
        zl[f] = ends[1:2]

    for f in range(24):
        put(fields, f, f)
    xf[24] = velocity[0, 0].astype(BF16)
    xl[24] = velocity[0, 7].astype(BF16)
    for x in range(8):
        yf[24, x : x + 1] = velocity[1, x, 0:1]
        yl[24, x : x + 1] = velocity[1, x, 31:32]
    ends = z_ends(velocity[2].reshape(256, 128))
    zf[24] = ends[0:1]
    zl[24] = ends[1:2]


def section_kernel(kind, *refs):
    refs = list(refs)
    q = refs.pop(0)
    start = q if kind == 1 else refs.pop(0)
    xlo, xhi, ylo, yhi, zlo, zhi = refs[:6]
    del refs[:6]
    if kind == 1:
        velocity, vxlo, vxhi, vylo, vyhi, vzlo, vzhi = refs[:7]
        del refs[:7]
    else:
        coef = refs.pop(0)
    out = refs.pop(0)
    if kind == 1:
        coef = refs.pop(0)
    if kind < 3:
        xf, xl, yf, yl, zf, zl = refs[:6]
        del refs[:6]
    zcol = refs.pop(0)

    if kind == 1:

        @pl.when(pl.program_id(0) == 0)
        def _():
            zcol[0] = z_columns(vzlo[0], vzhi[0])
            for x in range(8):
                before = vxlo[0].astype(F32) if x == 0 else velocity[0, x - 1]
                after = vxhi[0].astype(F32) if x == 7 else velocity[0, x + 1]
                y_next, y_prev, _, _ = shifted(
                    velocity[1, x], vylo[0, x : x + 1], vyhi[0, x : x + 1], velocity[1, x]
                )
                _, _, z_next, z_prev = shifted(
                    velocity[2, x], vylo[0, x : x + 1], vyhi[0, x : x + 1], zcol[0, 32 * x : 32 * x + 32]
                )
                coef[0, x] = 0.05 - 0.5 * after
                coef[1, x] = 0.05 + 0.5 * before
                coef[2, x] = 0.05 - 0.5 * y_next
                coef[3, x] = 0.05 + 0.5 * y_prev
                coef[4, x] = 0.05 - 0.5 * z_next
                coef[5, x] = 0.05 + 0.5 * z_prev

    for f in range(GROUP):
        zcol[f] = z_columns(zlo[f], zhi[f])
    for x in range(8):
        ce = [coef[i, x] for i in range(6)]
        for f in range(GROUP):
            centre = q[f, x]
            before = xlo[f].astype(F32) if x == 0 else q[f, x - 1]
            after = xhi[f].astype(F32) if x == 7 else q[f, x + 1]
            y_next, y_prev, z_next, z_prev = shifted(
                centre, ylo[f, x : x + 1], yhi[f, x : x + 1], zcol[f, 32 * x : 32 * x + 32]
            )
            moved = (
                0.7 * centre
                + (ce[0] * after + ce[1] * before)
                + (ce[2] * y_next + ce[3] * y_prev)
                + (ce[4] * z_next + ce[5] * z_prev)
            )
            if kind == 1:
                new = moved
            elif kind == 2:
                new = 0.75 * start[f, x] + 0.25 * moved
            else:
                new = (1.0 / 3.0) * start[f, x] + (2.0 / 3.0) * moved
            out[f, x] = new
            if kind < 3:
                put_faces(new, f, x, xf, xl, yf, yl)
    if kind < 3:
        for f in range(GROUP):
            put_z_faces(out, f, zf, zl)


def diffuse_kernel(rates, q, xlo, xhi, ylo, yhi, zlo, zhi, heats, out, activity, zcol):
    @pl.when(pl.program_id(0) == 0)
    def _():
        activity[0, 0] = jnp.sum(heats[...]) * (1.0 / (8.0 * 128.0))

    base = pl.program_id(0) * GROUP
    for f in range(GROUP):
        zcol[f] = z_columns(zlo[f], zhi[f])
        rate = rates[base + f]
        for x in range(8):
            centre = q[f, x]
            before = xlo[f].astype(F32) if x == 0 else q[f, x - 1]
            after = xhi[f].astype(F32) if x == 7 else q[f, x + 1]
            y_next, y_prev, z_next, z_prev = shifted(
                centre, ylo[f, x : x + 1], yhi[f, x : x + 1], zcol[f, 32 * x : 32 * x + 32]
            )
            spread = (after + before) + (y_next + y_prev) + (z_next + z_prev) - 6.0 * centre
            out[f, x] = centre + rate * spread


def columns_kernel(w_in, b_in, w_mid, w_low, b_mid, b_low, b_out, w1, w2, w3, b2, b3, b4):
    bias = 0.5 * b_in[...]
    parts = []
    for _ in range(3):
        parts.append(bias.astype(BF16).astype(F32))
        bias = bias - parts[-1]
    zeros = jnp.zeros((5, bias.shape[1]), F32)
    w1[...] = jnp.concatenate([0.5 * w_in[...].astype(F32), *parts, zeros], axis=0).T.astype(BF16)
    w2[...] = (0.5 * w_mid[...].astype(F32)).astype(BF16)
    w3[...] = (0.5 * w_low[...].astype(F32)).astype(BF16)
    for row, out, factor in ((b_mid, b2, 0.5), (b_low, b3, 0.5), (b_out, b4, 1.0)):
        out[...] = jnp.broadcast_to(factor * row[...], (128, row.shape[1])).T


def network_kernel(listed, flowed, owned_by, w1, w2, w3, b2, b3, b4, w4, out, sent, xf, xl, yf, yl, zf, zl, heat):
    def copy(f, carry):
        rows = pl.ds(pl.multiple_of(256 * f, 256), 256)
        out[rows, :] = flowed[rows, :]
        return carry

    def product(weights, cells):
        return jnp.dot(weights[...], cells, preferred_element_type=F32)

    def beside(bias):
        return jnp.concatenate([bias[...]] * TOGETHER, axis=1)

    def silu(half):
        return (half + half * jnp.tanh(half)).astype(BF16)

    def react(step, carry):
        first = step * TOGETHER
        rows = [pl.ds(listed[1 + first + j], 24, stride=256) for j in range(TOGETHER)]
        before = [flowed[r, :] for r in rows]
        ones = jnp.ones((8, TOGETHER * 128), F32)
        cells = jnp.concatenate([jnp.concatenate(before, axis=1), ones], axis=0).astype(BF16)
        hidden = silu(product(w1, cells))
        hidden = silu(product(w2, hidden) + beside(b2))
        hidden = silu(product(w3, hidden) + beside(b3))
        result = product(w4, hidden) + beside(b4)
        for j in range(TOGETHER):
            increment = result[:, 128 * j : 128 * j + 128]
            out[rows[j], :] = before[j] + increment
            heat[pl.ds(first + j, 1), :] = increment[0:1] * increment[0:1]
        return carry

    def faces(f, carry):
        base = pl.multiple_of(256 * f, 256)
        xf[f] = out[pl.ds(base, 32), :].astype(BF16)
        xl[f] = out[pl.ds(base + 224, 32), :].astype(BF16)
        yf[f] = out[pl.ds(base, 8, stride=32), :]
        yl[f] = out[pl.ds(base + 31, 8, stride=32), :]
        ends = z_ends(out[pl.ds(base, 256), :])
        zf[f] = ends[0:1]
        zl[f] = ends[1:2]
        return carry

    heat[...] = jnp.zeros_like(heat)
    lax.fori_loop(0, 24, copy, 0)
    lax.fori_loop(0, (listed[0] + TOGETHER - 1) // TOGETHER, react, 0)
    lax.fori_loop(0, 24, faces, 0)
    sent[...] = jnp.dot(
        owned_by[...], heat[...], preferred_element_type=F32, precision=lax.Precision.HIGHEST
    )


def params(mib):
    return pltpu.CompilerParams(vmem_limit_bytes=mib * 1024 * 1024)


def sds(shape, dtype):
    return jax.ShapeDtypeStruct(shape, dtype)


def whole(shape):
    return pl.BlockSpec(shape, lambda *_: (0,) * len(shape))


def at(shape, place):
    return pl.BlockSpec(shape, lambda *_: place)


BRICK = pl.BlockSpec((GROUP, 8, 32, 128), lambda g, *_: (g, 0, 0, 0))
X_FACE = pl.BlockSpec((GROUP, 32, 128), lambda g, *_: (g, 0, 0))
Y_FACE = pl.BlockSpec((GROUP, 8, 128), lambda g, *_: (g, 0, 0))
Z_FACE = pl.BlockSpec((GROUP, 1, 256), lambda g, *_: (g, 0, 0))
FACES = [X_FACE, X_FACE, Y_FACE, Y_FACE, Z_FACE, Z_FACE]


def face_shapes(count):
    return [
        sds((count, 32, 128), BF16),
        sds((count, 32, 128), BF16),
        sds((count, 8, 128), F32),
        sds((count, 8, 128), F32),
        sds((count, 1, 256), F32),
        sds((count, 1, 256), F32),
    ]


def exchange(faces):
    got = []
    for axis, first, last in zip(ALL, faces[0::2], faces[1::2]):
        n = lax.axis_size(axis)
        got.append(lax.ppermute(last, axis, [(i, (i + 1) % n) for i in range(n)]))
        got.append(lax.ppermute(first, axis, [((i + 1) % n, i) for i in range(n)]))
    return got


def section(kind, args, in_specs, out_shapes, out_specs):
    return pl.pallas_call(
        functools.partial(section_kernel, kind),
        grid=(24 // GROUP,),
        in_specs=in_specs,
        out_specs=out_specs,
        out_shape=out_shapes,
        scratch_shapes=[pltpu.VMEM((GROUP, 256, 128), F32)],
        compiler_params=params(32),
    )(*args)


def swap(tiles):
    return lax.all_to_all(tiles, ALL, split_axis=0, concat_axis=0, tiled=True)


def local(
    fields,
    velocity,
    diffusivity,
    weight_in,
    bias_in,
    weight_mid,
    bias_mid,
    weight_low,
    bias_low,
    weight_out,
    bias_out,
    react_list,
    owner_table,
):
    brick = sds(fields.shape, F32)
    ids, owners = react_list[0], owner_table[0]
    count = jnp.sum((ids >= 0).astype(jnp.int32))
    listed = jnp.concatenate([count[None], jnp.where(ids >= 0, ids, ids[0])])
    owned_by = (owners[None, :] == jnp.arange(128, dtype=jnp.int32)[:, None]).astype(F32)

    faces = pl.pallas_call(
        prep_kernel, out_shape=face_shapes(25), compiler_params=params(32)
    )(fields, velocity)
    halo = exchange(faces)
    own_halo = [
        at((1, 32, 128), (24, 0, 0)),
        at((1, 32, 128), (24, 0, 0)),
        at((1, 8, 128), (24, 0, 0)),
        at((1, 8, 128), (24, 0, 0)),
        at((1, 1, 256), (24, 0, 0)),
        at((1, 1, 256), (24, 0, 0)),
    ]
    one, coef, *faces = section(
        1,
        (fields, *halo, velocity, *halo),
        [BRICK, *FACES, whole((3, 8, 32, 128)), *own_halo],
        [brick, sds((6, 8, 32, 128), F32), *face_shapes(24)],
        [BRICK, whole((6, 8, 32, 128)), *FACES],
    )
    one, *given = lax.optimization_barrier(
        (
            one,
            weight_in,
            bias_in.reshape(1, -1),
            weight_mid.T,
            weight_low.T,
            *(b.reshape(1, -1) for b in (bias_mid, bias_low, bias_out)),
        )
    )
    columns = pl.pallas_call(
        columns_kernel,
        out_shape=[
            sds((weight_in.shape[1], 32), BF16),
            sds(weight_mid.shape[::-1], BF16),
            sds(weight_low.shape[::-1], BF16),
            *(sds((b.shape[0], 128), F32) for b in (bias_mid, bias_low, bias_out)),
        ],
        compiler_params=params(20),
        cost_estimate=pl.CostEstimate(flops=0, bytes_accessed=8 * 2**20, transcendentals=0),
    )(*given)
    two, *faces = section(
        2,
        (one, fields, *exchange(faces), coef),
        [BRICK, BRICK, *FACES, whole((6, 8, 32, 128))],
        [brick, *face_shapes(24)],
        [BRICK, *FACES],
    )
    (flowed,) = section(
        3,
        (two, fields, *exchange(faces), coef),
        [BRICK, BRICK, *FACES, whole((6, 8, 32, 128))],
        [brick],
        [BRICK],
    )
    in_vmem = pl.BlockSpec(memory_space=pltpu.VMEM)
    reacted, sent, *faces = pl.pallas_call(
        network_kernel,
        in_specs=[pl.BlockSpec(memory_space=pltpu.SMEM)] + [in_vmem] * 9,
        out_specs=[in_vmem] * 8,
        out_shape=[sds((24 * 256, 128), F32), sds((128, 128), F32), *face_shapes(24)],
        scratch_shapes=[pltpu.VMEM((LISTED, 128), F32)],
        compiler_params=params(NETWORK_MIB),
    )(listed, flowed.reshape(24 * 256, 128), owned_by, *columns, weight_out.T)
    reacted = reacted.reshape(fields.shape)
    around = exchange(faces)
    heats = swap(sent.reshape(128, 1, 128)).reshape(128, 128)
    updated, activity = pl.pallas_call(
        diffuse_kernel,
        grid=(24 // GROUP,),
        in_specs=[pl.BlockSpec(memory_space=pltpu.SMEM), BRICK, *FACES, whole((128, 128))],
        out_specs=[BRICK, pl.BlockSpec(memory_space=pltpu.SMEM)],
        out_shape=[brick, sds((1, 1), F32)],
        scratch_shapes=[pltpu.VMEM((GROUP, 256, 128), F32)],
        compiler_params=params(32),
        cost_estimate=pl.CostEstimate(flops=10**9, bytes_accessed=24 * 2**20, transcendentals=0),
    )(diffusivity, reacted, *around, heats)
    return (updated, activity.reshape(1))


def solution(mesh):
    return jax.shard_map(
        local,
        mesh=mesh,
        in_specs=(
            P(None, *ALL),
            P(None, *ALL),
            *(P(),) * 9,
            P(ALL, None),
            P(ALL, None),
        ),
        out_specs=(P(None, *ALL), P(ALL)),
        check_vma=False,
    )
```

```python
import functools

import jax
import jax.numpy as jnp
from jax import lax
from jax.experimental import pallas as pl
from jax.experimental.pallas import tpu as pltpu
from jax.sharding import PartitionSpec as P

GROUP = 12
TOGETHER = 12
LISTED = 96
NETWORK_MIB = 38
ALL = ("gx", "gy", "gz")
F32, BF16 = jnp.float32, jnp.bfloat16
TN = (((0,), (0,)), ((), ()))
NT = (((1,), (1,)), ((), ()))


def one_hot_ends():
    rows = lax.broadcasted_iota(jnp.int32, (16, 128), 0)
    lanes = lax.broadcasted_iota(jnp.int32, (16, 128), 1)
    return (((rows == 0) & (lanes == 0)) | ((rows == 1) & (lanes == 127))).astype(F32).astype(BF16)


def z_columns(low, high):
    rows = lax.broadcasted_iota(jnp.int32, (16, 256), 0)
    pair = jnp.where(rows == 0, low, jnp.where(rows == 1, high, 0.0)).astype(BF16)
    return lax.dot_general(pair, one_hot_ends(), TN, preferred_element_type=F32)


def z_ends(cells):
    return lax.dot_general(one_hot_ends(), cells.astype(BF16), NT, preferred_element_type=F32)


def shifted(centre, y_low, y_high, z_col):
    rows = lax.broadcasted_iota(jnp.int32, (32, 128), 0)
    lanes = lax.broadcasted_iota(jnp.int32, (32, 128), 1)
    y_next = jnp.where(rows == 31, y_high, pltpu.roll(centre, 31, 0))
    y_prev = jnp.where(rows == 0, y_low, pltpu.roll(centre, 1, 0))
    z_next = jnp.where(lanes == 127, z_col, pltpu.roll(centre, 127, 1))
    z_prev = jnp.where(lanes == 0, z_col, pltpu.roll(centre, 1, 1))
    return y_next, y_prev, z_next, z_prev


def put_faces(new, f, x, xf, xl, yf, yl):
    if x == 0:
        xf[f] = new.astype(BF16)
    if x == 7:
        xl[f] = new.astype(BF16)
    yf[f, x : x + 1] = new[0:1]
    yl[f, x : x + 1] = new[31:32]


def put_z_faces(out, f, zf, zl):
    ends = z_ends(out[f].reshape(256, 128))
    zf[f] = ends[0:1]
    zl[f] = ends[1:2]


def prep_kernel(fields, velocity, xf, xl, yf, yl, zf, zl):
    def put(ref, i, f):
        xf[f] = ref[i, 0].astype(BF16)
        xl[f] = ref[i, 7].astype(BF16)
        for x in range(8):
            yf[f, x : x + 1] = ref[i, x, 0:1]
            yl[f, x : x + 1] = ref[i, x, 31:32]
        ends = z_ends(ref[i].reshape(256, 128))
        zf[f] = ends[0:1]
        zl[f] = ends[1:2]

    for f in range(24):
        put(fields, f, f)
    xf[24] = velocity[0, 0].astype(BF16)
    xl[24] = velocity[0, 7].astype(BF16)
    for x in range(8):
        yf[24, x : x + 1] = velocity[1, x, 0:1]
        yl[24, x : x + 1] = velocity[1, x, 31:32]
    ends = z_ends(velocity[2].reshape(256, 128))
    zf[24] = ends[0:1]
    zl[24] = ends[1:2]


def section_kernel(kind, *refs):
    refs = list(refs)
    q = refs.pop(0)
    start = q if kind == 1 else refs.pop(0)
    xlo, xhi, ylo, yhi, zlo, zhi = refs[:6]
    del refs[:6]
    if kind == 1:
        velocity, vxlo, vxhi, vylo, vyhi, vzlo, vzhi = refs[:7]
        del refs[:7]
    else:
        coef = refs.pop(0)
    out = refs.pop(0)
    if kind == 1:
        coef = refs.pop(0)
    if kind < 3:
        xf, xl, yf, yl, zf, zl = refs[:6]
        del refs[:6]
    zcol = refs.pop(0)

    if kind == 1:

        @pl.when(pl.program_id(0) == 0)
        def _():
            zcol[0] = z_columns(vzlo[0], vzhi[0])
            for x in range(8):
                before = vxlo[0].astype(F32) if x == 0 else velocity[0, x - 1]
                after = vxhi[0].astype(F32) if x == 7 else velocity[0, x + 1]
                y_next, y_prev, _, _ = shifted(
                    velocity[1, x], vylo[0, x : x + 1], vyhi[0, x : x + 1], velocity[1, x]
                )
                _, _, z_next, z_prev = shifted(
                    velocity[2, x], vylo[0, x : x + 1], vyhi[0, x : x + 1], zcol[0, 32 * x : 32 * x + 32]
                )
                coef[0, x] = 0.05 - 0.5 * after
                coef[1, x] = 0.05 + 0.5 * before
                coef[2, x] = 0.05 - 0.5 * y_next
                coef[3, x] = 0.05 + 0.5 * y_prev
                coef[4, x] = 0.05 - 0.5 * z_next
                coef[5, x] = 0.05 + 0.5 * z_prev

    for f in range(GROUP):
        zcol[f] = z_columns(zlo[f], zhi[f])
    for x in range(8):
        ce = [coef[i, x] for i in range(6)]
        for f in range(GROUP):
            centre = q[f, x]
            before = xlo[f].astype(F32) if x == 0 else q[f, x - 1]
            after = xhi[f].astype(F32) if x == 7 else q[f, x + 1]
            y_next, y_prev, z_next, z_prev = shifted(
                centre, ylo[f, x : x + 1], yhi[f, x : x + 1], zcol[f, 32 * x : 32 * x + 32]
            )
            moved = (
                0.7 * centre
                + (ce[0] * after + ce[1] * before)
                + (ce[2] * y_next + ce[3] * y_prev)
                + (ce[4] * z_next + ce[5] * z_prev)
            )
            if kind == 1:
                new = moved
            elif kind == 2:
                new = 0.75 * start[f, x] + 0.25 * moved
            else:
                new = (1.0 / 3.0) * start[f, x] + (2.0 / 3.0) * moved
            out[f, x] = new
            if kind < 3:
                put_faces(new, f, x, xf, xl, yf, yl)
    if kind < 3:
        for f in range(GROUP):
            put_z_faces(out, f, zf, zl)


def diffuse_kernel(rates, q, xlo, xhi, ylo, yhi, zlo, zhi, heats, out, activity, zcol):
    @pl.when(pl.program_id(0) == 0)
    def _():
        activity[0, 0] = jnp.sum(heats[...]) * (1.0 / (8.0 * 128.0))

    base = pl.program_id(0) * GROUP
    for f in range(GROUP):
        zcol[f] = z_columns(zlo[f], zhi[f])
        rate = rates[base + f]
        for x in range(8):
            centre = q[f, x]
            before = xlo[f].astype(F32) if x == 0 else q[f, x - 1]
            after = xhi[f].astype(F32) if x == 7 else q[f, x + 1]
            y_next, y_prev, z_next, z_prev = shifted(
                centre, ylo[f, x : x + 1], yhi[f, x : x + 1], zcol[f, 32 * x : 32 * x + 32]
            )
            spread = (after + before) + (y_next + y_prev) + (z_next + z_prev) - 6.0 * centre
            out[f, x] = centre + rate * spread


def columns_kernel(w_in, b_in, w_mid, w_low, b_mid, b_low, b_out, w1, w2, w3, b2, b3, b4):
    bias = 0.5 * b_in[...]
    parts = []
    for _ in range(3):
        parts.append(bias.astype(BF16).astype(F32))
        bias = bias - parts[-1]
    zeros = jnp.zeros((5, bias.shape[1]), F32)
    w1[...] = jnp.concatenate([0.5 * w_in[...].astype(F32), *parts, zeros], axis=0).T.astype(BF16)
    w2[...] = (0.5 * w_mid[...].astype(F32)).astype(BF16)
    w3[...] = (0.5 * w_low[...].astype(F32)).astype(BF16)
    for row, out, factor in ((b_mid, b2, 0.5), (b_low, b3, 0.5), (b_out, b4, 1.0)):
        out[...] = jnp.broadcast_to(factor * row[...], (128, row.shape[1])).T


def network_kernel(listed, flowed, owned_by, w1, w2, w3, b2, b3, b4, w4, out, sent, xf, xl, yf, yl, zf, zl, heat):
    def copy(part, carry):
        rows = pl.ds(pl.multiple_of(part * 1536, 1536), 1536)
        out[rows, :] = flowed[rows, :]
        return carry

    def block(i):
        return jnp.where(listed[0, i] < 0, listed[0, 0], listed[0, i])

    def product(weights, cells):
        return jnp.dot(weights[...], cells, preferred_element_type=F32)

    def beside(bias):
        return jnp.concatenate([bias[...]] * TOGETHER, axis=1)

    def silu(half):
        return (half + half * jnp.tanh(half)).astype(BF16)

    def react(step, carry):
        first = step * TOGETHER
        rows = [pl.ds(block(first + j), 24, stride=256) for j in range(TOGETHER)]
        before = [flowed[r, :] for r in rows]
        ones = jnp.ones((8, TOGETHER * 128), F32)
        cells = jnp.concatenate([jnp.concatenate(before, axis=1), ones], axis=0).astype(BF16)
        hidden = silu(product(w1, cells))
        hidden = silu(product(w2, hidden) + beside(b2))
        hidden = silu(product(w3, hidden) + beside(b3))
        result = product(w4, hidden) + beside(b4)
        for j in range(TOGETHER):
            increment = result[:, 128 * j : 128 * j + 128]
            out[rows[j], :] = before[j] + increment
            heat[pl.ds(first + j, 1), :] = increment[0:1] * increment[0:1]
        return carry

    def faces(part, carry):
        ends = z_ends(out[pl.ds(pl.multiple_of(part * 1536, 1536), 1536), :])
        for j in range(6):
            f = 6 * part + j
            base = pl.multiple_of(256 * f, 256)
            xf[f] = out[pl.ds(base, 32), :].astype(BF16)
            xl[f] = out[pl.ds(base + 224, 32), :].astype(BF16)
            yf[f] = out[pl.ds(base, 8, stride=32), :]
            yl[f] = out[pl.ds(base + 31, 8, stride=32), :]
            zf[f] = ends[0:1, 256 * j : 256 * j + 256]
            zl[f] = ends[1:2, 256 * j : 256 * j + 256]
        return carry

    heat[...] = jnp.zeros_like(heat)
    lax.fori_loop(0, 4, copy, 0)
    count = lax.fori_loop(0, LISTED, lambda i, n: n + jnp.where(listed[0, i] < 0, 0, 1), 0)
    lax.fori_loop(0, (count + TOGETHER - 1) // TOGETHER, react, 0)
    lax.fori_loop(0, 4, faces, 0)
    sent[...] = jnp.dot(
        owned_by[...], heat[...], preferred_element_type=F32, precision=lax.Precision.HIGHEST
    )


def params(mib):
    return pltpu.CompilerParams(vmem_limit_bytes=mib * 1024 * 1024)


def sds(shape, dtype):
    return jax.ShapeDtypeStruct(shape, dtype)


def whole(shape):
    return pl.BlockSpec(shape, lambda *_: (0,) * len(shape))


def at(shape, place):
    return pl.BlockSpec(shape, lambda *_: place)


BRICK = pl.BlockSpec((GROUP, 8, 32, 128), lambda g, *_: (g, 0, 0, 0))
X_FACE = pl.BlockSpec((GROUP, 32, 128), lambda g, *_: (g, 0, 0))
Y_FACE = pl.BlockSpec((GROUP, 8, 128), lambda g, *_: (g, 0, 0))
Z_FACE = pl.BlockSpec((GROUP, 1, 256), lambda g, *_: (g, 0, 0))
FACES = [X_FACE, X_FACE, Y_FACE, Y_FACE, Z_FACE, Z_FACE]


def face_shapes(count):
    return [
        sds((count, 32, 128), BF16),
        sds((count, 32, 128), BF16),
        sds((count, 8, 128), F32),
        sds((count, 8, 128), F32),
        sds((count, 1, 256), F32),
        sds((count, 1, 256), F32),
    ]


def exchange(faces):
    got = []
    for axis, first, last in zip(ALL, faces[0::2], faces[1::2]):
        n = lax.axis_size(axis)
        got.append(lax.ppermute(last, axis, [(i, (i + 1) % n) for i in range(n)]))
        got.append(lax.ppermute(first, axis, [((i + 1) % n, i) for i in range(n)]))
    return got


def section(kind, args, in_specs, out_shapes, out_specs):
    return pl.pallas_call(
        functools.partial(section_kernel, kind),
        grid=(24 // GROUP,),
        in_specs=in_specs,
        out_specs=out_specs,
        out_shape=out_shapes,
        scratch_shapes=[pltpu.VMEM((GROUP, 256, 128), F32)],
        compiler_params=params(32),
    )(*args)


def swap(tiles):
    return lax.all_to_all(tiles, ALL, split_axis=0, concat_axis=0, tiled=True)


def local(
    fields,
    velocity,
    diffusivity,
    weight_in,
    bias_in,
    weight_mid,
    bias_mid,
    weight_low,
    bias_low,
    weight_out,
    bias_out,
    react_list,
    owner_table,
):
    brick = sds(fields.shape, F32)
    owners = owner_table[0]
    owned_by = (owners[None, :] == jnp.arange(128, dtype=jnp.int32)[:, None]).astype(F32)

    faces = pl.pallas_call(
        prep_kernel, out_shape=face_shapes(25), compiler_params=params(32)
    )(fields, velocity)
    halo = exchange(faces)
    own_halo = [
        at((1, 32, 128), (24, 0, 0)),
        at((1, 32, 128), (24, 0, 0)),
        at((1, 8, 128), (24, 0, 0)),
        at((1, 8, 128), (24, 0, 0)),
        at((1, 1, 256), (24, 0, 0)),
        at((1, 1, 256), (24, 0, 0)),
    ]
    one, coef, *faces = section(
        1,
        (fields, *halo, velocity, *halo),
        [BRICK, *FACES, whole((3, 8, 32, 128)), *own_halo],
        [brick, sds((6, 8, 32, 128), F32), *face_shapes(24)],
        [BRICK, whole((6, 8, 32, 128)), *FACES],
    )
    one, *given = lax.optimization_barrier(
        (
            one,
            weight_in,
            bias_in.reshape(1, -1),
            weight_mid.T,
            weight_low.T,
            *(b.reshape(1, -1) for b in (bias_mid, bias_low, bias_out)),
        )
    )
    columns = pl.pallas_call(
        columns_kernel,
        out_shape=[
            sds((weight_in.shape[1], 32), BF16),
            sds(weight_mid.shape[::-1], BF16),
            sds(weight_low.shape[::-1], BF16),
            *(sds((b.shape[0], 128), F32) for b in (bias_mid, bias_low, bias_out)),
        ],
        compiler_params=params(20),
        cost_estimate=pl.CostEstimate(flops=0, bytes_accessed=8 * 2**20, transcendentals=0),
    )(*given)
    two, *faces = section(
        2,
        (one, fields, *exchange(faces), coef),
        [BRICK, BRICK, *FACES, whole((6, 8, 32, 128))],
        [brick, *face_shapes(24)],
        [BRICK, *FACES],
    )
    (flowed,) = section(
        3,
        (two, fields, *exchange(faces), coef),
        [BRICK, BRICK, *FACES, whole((6, 8, 32, 128))],
        [brick],
        [BRICK],
    )
    in_vmem = pl.BlockSpec(memory_space=pltpu.VMEM)
    reacted, sent, *faces = pl.pallas_call(
        network_kernel,
        in_specs=[pl.BlockSpec(memory_space=pltpu.SMEM)] + [in_vmem] * 9,
        out_specs=[in_vmem] * 8,
        out_shape=[sds((24 * 256, 128), F32), sds((128, 128), F32), *face_shapes(24)],
        scratch_shapes=[pltpu.VMEM((LISTED, 128), F32)],
        compiler_params=params(NETWORK_MIB),
    )(react_list, flowed.reshape(24 * 256, 128), owned_by, *columns, weight_out.T)
    reacted = reacted.reshape(fields.shape)
    around = exchange(faces)
    heats = swap(sent.reshape(128, 1, 128)).reshape(128, 128)
    updated, activity = pl.pallas_call(
        diffuse_kernel,
        grid=(24 // GROUP,),
        in_specs=[pl.BlockSpec(memory_space=pltpu.SMEM), BRICK, *FACES, whole((128, 128))],
        out_specs=[BRICK, pl.BlockSpec(memory_space=pltpu.SMEM)],
        out_shape=[brick, sds((1, 1), F32)],
        scratch_shapes=[pltpu.VMEM((GROUP, 256, 128), F32)],
        compiler_params=params(32),
        cost_estimate=pl.CostEstimate(flops=10**9, bytes_accessed=24 * 2**20, transcendentals=0),
    )(diffusivity, reacted, *around, heats)
    return (updated, activity.reshape(1))


def solution(mesh):
    return jax.shard_map(
        local,
        mesh=mesh,
        in_specs=(
            P(None, *ALL),
            P(None, *ALL),
            *(P(),) * 9,
            P(ALL, None),
            P(ALL, None),
        ),
        out_specs=(P(None, *ALL), P(ALL)),
        check_vma=False,
    )
```

```python
import functools

import jax
import jax.numpy as jnp
from jax import lax
from jax.experimental import pallas as pl
from jax.experimental.pallas import tpu as pltpu
from jax.sharding import PartitionSpec as P

GROUP = 12
TOGETHER = 12
LISTED = 96
NETWORK_MIB = 38
ALL = ("gx", "gy", "gz")
F32, BF16 = jnp.float32, jnp.bfloat16
TN = (((0,), (0,)), ((), ()))
NT = (((1,), (1,)), ((), ()))


def one_hot_ends():
    rows = lax.broadcasted_iota(jnp.int32, (16, 128), 0)
    lanes = lax.broadcasted_iota(jnp.int32, (16, 128), 1)
    return (((rows == 0) & (lanes == 0)) | ((rows == 1) & (lanes == 127))).astype(F32).astype(BF16)


def z_columns(low, high):
    rows = lax.broadcasted_iota(jnp.int32, (16, 256), 0)
    pair = jnp.where(rows == 0, low, jnp.where(rows == 1, high, 0.0)).astype(BF16)
    return lax.dot_general(pair, one_hot_ends(), TN, preferred_element_type=F32)


def z_ends(cells):
    return lax.dot_general(one_hot_ends(), cells.astype(BF16), NT, preferred_element_type=F32)


def shifted(centre, y_low, y_high, z_col):
    rows = lax.broadcasted_iota(jnp.int32, (32, 128), 0)
    lanes = lax.broadcasted_iota(jnp.int32, (32, 128), 1)
    y_next = jnp.where(rows == 31, y_high, pltpu.roll(centre, 31, 0))
    y_prev = jnp.where(rows == 0, y_low, pltpu.roll(centre, 1, 0))
    z_next = jnp.where(lanes == 127, z_col, pltpu.roll(centre, 127, 1))
    z_prev = jnp.where(lanes == 0, z_col, pltpu.roll(centre, 1, 1))
    return y_next, y_prev, z_next, z_prev


def put_faces(new, f, x, xf, xl, yf, yl):
    if x == 0:
        xf[f] = new.astype(BF16)
    if x == 7:
        xl[f] = new.astype(BF16)
    yf[f, x : x + 1] = new[0:1]
    yl[f, x : x + 1] = new[31:32]


def put_z_faces(out, f, zf, zl):
    ends = z_ends(out[f].reshape(256, 128))
    zf[f] = ends[0:1]
    zl[f] = ends[1:2]


def prep_kernel(fields, velocity, xf, xl, yf, yl, zf, zl):
    def put(ref, i, f):
        xf[f] = ref[i, 0].astype(BF16)
        xl[f] = ref[i, 7].astype(BF16)
        for x in range(8):
            yf[f, x : x + 1] = ref[i, x, 0:1]
            yl[f, x : x + 1] = ref[i, x, 31:32]
        ends = z_ends(ref[i].reshape(256, 128))
        zf[f] = ends[0:1]
        zl[f] = ends[1:2]

    for f in range(24):
        put(fields, f, f)
    xf[24] = velocity[0, 0].astype(BF16)
    xl[24] = velocity[0, 7].astype(BF16)
    for x in range(8):
        yf[24, x : x + 1] = velocity[1, x, 0:1]
        yl[24, x : x + 1] = velocity[1, x, 31:32]
    ends = z_ends(velocity[2].reshape(256, 128))
    zf[24] = ends[0:1]
    zl[24] = ends[1:2]


def section_kernel(kind, *refs):
    refs = list(refs)
    q = refs.pop(0)
    start = q if kind == 1 else refs.pop(0)
    xlo, xhi, ylo, yhi, zlo, zhi = refs[:6]
    del refs[:6]
    if kind == 1:
        velocity, vxlo, vxhi, vylo, vyhi, vzlo, vzhi = refs[:7]
        del refs[:7]
    else:
        coef = refs.pop(0)
    out = refs.pop(0)
    if kind == 1:
        coef = refs.pop(0)
    if kind < 3:
        xf, xl, yf, yl, zf, zl = refs[:6]
        del refs[:6]
    zcol = refs.pop(0)

    if kind == 1:
        zcol[0] = z_columns(vzlo[24], vzhi[24])
        for x in range(8):
            before = vxlo[24].astype(F32) if x == 0 else velocity[0, x - 1]
            after = vxhi[24].astype(F32) if x == 7 else velocity[0, x + 1]
            y_next, y_prev, _, _ = shifted(
                velocity[1, x], vylo[24, x : x + 1], vyhi[24, x : x + 1], velocity[1, x]
            )
            _, _, z_next, z_prev = shifted(
                velocity[2, x], vylo[24, x : x + 1], vyhi[24, x : x + 1], zcol[0, 32 * x : 32 * x + 32]
            )
            coef[0, x] = 0.05 - 0.5 * after
            coef[1, x] = 0.05 + 0.5 * before
            coef[2, x] = 0.05 - 0.5 * y_next
            coef[3, x] = 0.05 + 0.5 * y_prev
            coef[4, x] = 0.05 - 0.5 * z_next
            coef[5, x] = 0.05 + 0.5 * z_prev

    def part(p, carry):
        fs = [p * GROUP + i for i in range(GROUP)]
        for i, f in enumerate(fs):
            zcol[i] = z_columns(zlo[f], zhi[f])
        for x in range(8):
            ce = [coef[i, x] for i in range(6)]
            for i, f in enumerate(fs):
                centre = q[f, x]
                before = xlo[f].astype(F32) if x == 0 else q[f, x - 1]
                after = xhi[f].astype(F32) if x == 7 else q[f, x + 1]
                y_next, y_prev, z_next, z_prev = shifted(
                    centre, ylo[f, x : x + 1], yhi[f, x : x + 1], zcol[i, 32 * x : 32 * x + 32]
                )
                moved = (
                    0.7 * centre
                    + (ce[0] * after + ce[1] * before)
                    + (ce[2] * y_next + ce[3] * y_prev)
                    + (ce[4] * z_next + ce[5] * z_prev)
                )
                if kind == 1:
                    new = moved
                elif kind == 2:
                    new = 0.75 * start[f, x] + 0.25 * moved
                else:
                    new = (1.0 / 3.0) * start[f, x] + (2.0 / 3.0) * moved
                out[f, x] = new
                if kind < 3:
                    put_faces(new, f, x, xf, xl, yf, yl)
        if kind < 3:
            for f in fs:
                put_z_faces(out, f, zf, zl)
        return carry

    lax.fori_loop(0, 24 // GROUP, part, 0)


def diffuse_kernel(rates, q, xlo, xhi, ylo, yhi, zlo, zhi, heats, out, activity, zcol):
    activity[0, 0] = jnp.sum(heats[...]) * (1.0 / (8.0 * 128.0))

    def part(p, carry):
        for i in range(GROUP):
            f = p * GROUP + i
            zcol[i] = z_columns(zlo[f], zhi[f])
        for i in range(GROUP):
            f = p * GROUP + i
            rate = rates[pl.ds(f, 1), :]
            for x in range(8):
                centre = q[f, x]
                before = xlo[f].astype(F32) if x == 0 else q[f, x - 1]
                after = xhi[f].astype(F32) if x == 7 else q[f, x + 1]
                y_next, y_prev, z_next, z_prev = shifted(
                    centre, ylo[f, x : x + 1], yhi[f, x : x + 1], zcol[i, 32 * x : 32 * x + 32]
                )
                spread = (after + before) + (y_next + y_prev) + (z_next + z_prev) - 6.0 * centre
                out[f, x] = centre + rate * spread
        return carry

    lax.fori_loop(0, 24 // GROUP, part, 0)


def columns_kernel(
    w_in, b_in, w_mid, w_low, b_mid, b_low, b_out, diffusivity, w1, w2, w3, b2, b3, b4, rates
):
    bias = 0.5 * b_in[...]
    parts = []
    for _ in range(3):
        parts.append(bias.astype(BF16).astype(F32))
        bias = bias - parts[-1]
    zeros = jnp.zeros((5, bias.shape[1]), F32)
    w1[...] = jnp.concatenate([0.5 * w_in[...].astype(F32), *parts, zeros], axis=0).T.astype(BF16)
    w2[...] = (0.5 * w_mid[...].astype(F32)).astype(BF16)
    w3[...] = (0.5 * w_low[...].astype(F32)).astype(BF16)
    for row, out, factor in (
        (b_mid, b2, 0.5),
        (b_low, b3, 0.5),
        (b_out, b4, 1.0),
        (diffusivity, rates, 1.0),
    ):
        out[...] = jnp.broadcast_to(factor * row[...], (128, row.shape[1])).T


def network_kernel(listed, flowed, owned_by, w1, w2, w3, b2, b3, b4, w4, out, sent, xf, xl, yf, yl, zf, zl, heat):
    def copy(part, carry):
        rows = pl.ds(pl.multiple_of(part * 1536, 1536), 1536)
        out[rows, :] = flowed[rows, :]
        return carry

    def block(i):
        return jnp.where(listed[0, i] < 0, listed[0, 0], listed[0, i])

    def product(weights, cells):
        return jnp.dot(weights[...], cells, preferred_element_type=F32)

    def beside(bias):
        return jnp.concatenate([bias[...]] * TOGETHER, axis=1)

    def silu(half):
        return (half + half * jnp.tanh(half)).astype(BF16)

    def react(step, carry):
        first = step * TOGETHER
        rows = [pl.ds(block(first + j), 24, stride=256) for j in range(TOGETHER)]
        before = [flowed[r, :] for r in rows]
        ones = jnp.ones((8, TOGETHER * 128), F32)
        cells = jnp.concatenate([jnp.concatenate(before, axis=1), ones], axis=0).astype(BF16)
        hidden = silu(product(w1, cells))
        hidden = silu(product(w2, hidden) + beside(b2))
        hidden = silu(product(w3, hidden) + beside(b3))
        result = product(w4, hidden) + beside(b4)
        for j in range(TOGETHER):
            increment = result[:, 128 * j : 128 * j + 128]
            out[rows[j], :] = before[j] + increment
            heat[pl.ds(first + j, 1), :] = increment[0:1] * increment[0:1]
        return carry

    def faces(part, carry):
        ends = z_ends(out[pl.ds(pl.multiple_of(part * 1536, 1536), 1536), :])
        for j in range(6):
            f = 6 * part + j
            base = pl.multiple_of(256 * f, 256)
            xf[f] = out[pl.ds(base, 32), :].astype(BF16)
            xl[f] = out[pl.ds(base + 224, 32), :].astype(BF16)
            yf[f] = out[pl.ds(base, 8, stride=32), :]
            yl[f] = out[pl.ds(base + 31, 8, stride=32), :]
            zf[f] = ends[0:1, 256 * j : 256 * j + 256]
            zl[f] = ends[1:2, 256 * j : 256 * j + 256]
        return carry

    heat[...] = jnp.zeros_like(heat)
    lax.fori_loop(0, 4, copy, 0)
    count = lax.fori_loop(0, LISTED, lambda i, n: n + jnp.where(listed[0, i] < 0, 0, 1), 0)
    lax.fori_loop(0, (count + TOGETHER - 1) // TOGETHER, react, 0)
    lax.fori_loop(0, 4, faces, 0)
    sent[...] = jnp.dot(
        owned_by[...], heat[...], preferred_element_type=F32, precision=lax.Precision.HIGHEST
    )


def params(mib):
    return pltpu.CompilerParams(vmem_limit_bytes=mib * 1024 * 1024)


def sds(shape, dtype):
    return jax.ShapeDtypeStruct(shape, dtype)


IN_VMEM = pl.BlockSpec(memory_space=pltpu.VMEM)


def face_shapes(count):
    return [
        sds((count, 32, 128), BF16),
        sds((count, 32, 128), BF16),
        sds((count, 8, 128), F32),
        sds((count, 8, 128), F32),
        sds((count, 1, 256), F32),
        sds((count, 1, 256), F32),
    ]


def exchange(faces, axes=ALL):
    got = []
    for axis, first, last in zip(axes, faces[0::2], faces[1::2]):
        n = lax.axis_size(axis)
        got.append(lax.ppermute(last, axis, [(i, (i + 1) % n) for i in range(n)]))
        got.append(lax.ppermute(first, axis, [((i + 1) % n, i) for i in range(n)]))
    return got


def section(kind, args, out_shapes):
    return pl.pallas_call(
        functools.partial(section_kernel, kind),
        in_specs=[IN_VMEM] * len(args),
        out_specs=[IN_VMEM] * len(out_shapes),
        out_shape=out_shapes,
        scratch_shapes=[pltpu.VMEM((GROUP, 256, 128), F32)],
        compiler_params=params(24),
    )(*args)


def swap(tiles):
    return lax.all_to_all(tiles, ALL, split_axis=0, concat_axis=0, tiled=True)


def local(
    fields,
    velocity,
    diffusivity,
    weight_in,
    bias_in,
    weight_mid,
    bias_mid,
    weight_low,
    bias_low,
    weight_out,
    bias_out,
    react_list,
    owner_table,
):
    brick = sds(fields.shape, F32)
    owners = owner_table[0]
    owned_by = (owners[None, :] == jnp.arange(128, dtype=jnp.int32)[:, None]).astype(F32)

    faces = pl.pallas_call(
        prep_kernel, out_shape=face_shapes(25), compiler_params=params(32)
    )(fields, velocity)
    halo = exchange(faces)
    one, coef, *faces = section(
        1, (fields, *halo, velocity, *halo), [brick, sds((6, 8, 32, 128), F32), *face_shapes(24)]
    )
    one, *given = lax.optimization_barrier(
        (
            one,
            weight_in,
            bias_in.reshape(1, -1),
            weight_mid.T,
            weight_low.T,
            *(b.reshape(1, -1) for b in (bias_mid, bias_low, bias_out, diffusivity)),
        )
    )
    *columns, rates = pl.pallas_call(
        columns_kernel,
        out_shape=[
            sds((weight_in.shape[1], 32), BF16),
            sds(weight_mid.shape[::-1], BF16),
            sds(weight_low.shape[::-1], BF16),
            *(sds((b.shape[0], 128), F32) for b in (bias_mid, bias_low, bias_out, diffusivity)),
        ],
        compiler_params=params(20),
        cost_estimate=pl.CostEstimate(flops=0, bytes_accessed=8 * 2**20, transcendentals=0),
    )(*given)
    two, *faces = section(2, (one, fields, *exchange(faces), coef), [brick, *face_shapes(24)])
    (flowed,) = section(3, (two, fields, *exchange(faces), coef), [brick])
    reacted, sent, *faces = pl.pallas_call(
        network_kernel,
        in_specs=[pl.BlockSpec(memory_space=pltpu.SMEM)] + [IN_VMEM] * 9,
        out_specs=[IN_VMEM] * 8,
        out_shape=[sds((24 * 256, 128), F32), sds((128, 128), F32), *face_shapes(24)],
        scratch_shapes=[pltpu.VMEM((LISTED, 128), F32)],
        compiler_params=params(NETWORK_MIB),
    )(react_list, flowed.reshape(24 * 256, 128), owned_by, *columns, weight_out.T)
    reacted = reacted.reshape(fields.shape)
    x_and_y = exchange(faces[:4])
    *z_faces, x_and_y[0], x_and_y[1] = lax.optimization_barrier((*faces[4:], *x_and_y[:2]))
    around = x_and_y + exchange(z_faces, ALL[2:])
    heats = swap(sent.reshape(128, 1, 128)).reshape(128, 128)
    updated, activity = pl.pallas_call(
        diffuse_kernel,
        in_specs=[IN_VMEM] * 9,
        out_specs=[IN_VMEM, pl.BlockSpec(memory_space=pltpu.SMEM)],
        out_shape=[brick, sds((1, 1), F32)],
        scratch_shapes=[pltpu.VMEM((GROUP, 256, 128), F32)],
        compiler_params=params(24),
        cost_estimate=pl.CostEstimate(flops=10**9, bytes_accessed=24 * 2**20, transcendentals=0),
    )(rates, reacted, *around, heats)
    return (updated, activity.reshape(1))


def solution(mesh):
    return jax.shard_map(
        local,
        mesh=mesh,
        in_specs=(
            P(None, *ALL),
            P(None, *ALL),
            *(P(),) * 9,
            P(ALL, None),
            P(ALL, None),
        ),
        out_specs=(P(None, *ALL), P(ALL)),
        check_vma=False,
    )
```

```python
import functools

import jax
import jax.numpy as jnp
from jax import lax
from jax.experimental import pallas as pl
from jax.experimental.pallas import tpu as pltpu
from jax.sharding import PartitionSpec as P

GROUP = 24
LAST_GROUP = 8
TOGETHER = 12
LISTED = 96
NETWORK_MIB = 38
ALL = ("gx", "gy", "gz")
F32, BF16 = jnp.float32, jnp.bfloat16
TN = (((0,), (0,)), ((), ()))
NT = (((1,), (1,)), ((), ()))


def one_hot_ends():
    rows = lax.broadcasted_iota(jnp.int32, (16, 128), 0)
    lanes = lax.broadcasted_iota(jnp.int32, (16, 128), 1)
    return (((rows == 0) & (lanes == 0)) | ((rows == 1) & (lanes == 127))).astype(F32).astype(BF16)


def z_columns(low, high):
    rows = lax.broadcasted_iota(jnp.int32, (16, 256), 0)
    pair = jnp.where(rows == 0, low, jnp.where(rows == 1, high, 0.0)).astype(BF16)
    return lax.dot_general(pair, one_hot_ends(), TN, preferred_element_type=F32)


def all_z_columns(low, high):
    n = low.shape[0]
    rows = lax.broadcasted_iota(jnp.int32, (2 * n, 128 * n), 0)
    lanes = lax.broadcasted_iota(jnp.int32, (2 * n, 128 * n), 1)
    place = jnp.where(rows < n, 128 * rows, 128 * (rows - n) + 127)
    ends = (lanes == place).astype(F32).astype(BF16)
    pairs = jnp.concatenate([low, high], axis=0).astype(BF16)
    return lax.dot_general(pairs, ends, TN, preferred_element_type=F32)


def z_ends(cells):
    return lax.dot_general(one_hot_ends(), cells.astype(BF16), NT, preferred_element_type=F32)


def shifted(centre, y_low, y_high, z_col):
    rows = lax.broadcasted_iota(jnp.int32, (32, 128), 0)
    lanes = lax.broadcasted_iota(jnp.int32, (32, 128), 1)
    y_next = jnp.where(rows == 31, y_high, pltpu.roll(centre, 31, 0))
    y_prev = jnp.where(rows == 0, y_low, pltpu.roll(centre, 1, 0))
    z_next = jnp.where(lanes == 127, z_col, pltpu.roll(centre, 127, 1))
    z_prev = jnp.where(lanes == 0, z_col, pltpu.roll(centre, 1, 1))
    return y_next, y_prev, z_next, z_prev


def put_faces(new, f, x, xf, xl, yf, yl):
    if x == 0:
        xf[f] = new.astype(BF16)
    if x == 7:
        xl[f] = new.astype(BF16)
    yf[f, x : x + 1] = new[0:1]
    yl[f, x : x + 1] = new[31:32]


def put_z_faces(out, f, zf, zl):
    ends = z_ends(out[f].reshape(256, 128))
    zf[f : f + 1] = ends[0:1]
    zl[f : f + 1] = ends[1:2]


def x_faces_kernel(fields, velocity, xf, xl, planes, sems):
    copies = []
    for i, x in enumerate((0, 7)):
        copies.append(pltpu.make_async_copy(fields.at[:, x], planes.at[i, 0:24], sems.at[i, 0]))
        copies.append(pltpu.make_async_copy(velocity.at[0, x], planes.at[i, 24], sems.at[i, 1]))
    for copy in copies:
        copy.start()
    for copy in copies:
        copy.wait()
    xf[...] = planes[0].astype(BF16)
    xl[...] = planes[1].astype(BF16)


def prep_kernel(fields, velocity, yf, yl, zf, zl):
    for f in range(25):
        for x in range(8):
            cells = velocity[1, x] if f == 24 else fields[f, x]
            yf[f, x : x + 1] = cells[0:1]
            yl[f, x : x + 1] = cells[31:32]
        lines = velocity[2] if f == 24 else fields[f]
        ends = z_ends(lines.reshape(256, 128))
        zf[f : f + 1] = ends[0:1]
        zl[f : f + 1] = ends[1:2]


def section_kernel(kind, *refs):
    refs = list(refs)
    q = refs.pop(0)
    start = q if kind == 1 else refs.pop(0)
    xlo, xhi, ylo, yhi, zlo, zhi = refs[:6]
    del refs[:6]
    if kind == 1:
        velocity, vxlo, vxhi, vylo, vyhi, vzlo, vzhi = refs[:7]
        del refs[:7]
    else:
        coef = refs.pop(0)
    out = refs.pop(0)
    if kind == 1:
        coef = refs.pop(0)
    if kind < 3:
        xf, xl, yf, yl, zf, zl = refs[:6]
        del refs[:6]
    zcol = refs.pop(0)

    if kind == 1:
        v_col = z_columns(vzlo[24:25], vzhi[24:25])
        for x in range(8):
            before = vxlo[24].astype(F32) if x == 0 else velocity[0, x - 1]
            after = vxhi[24].astype(F32) if x == 7 else velocity[0, x + 1]
            y_next, y_prev, _, _ = shifted(
                velocity[1, x], vylo[24, x : x + 1], vyhi[24, x : x + 1], velocity[1, x]
            )
            _, _, z_next, z_prev = shifted(
                velocity[2, x], vylo[24, x : x + 1], vyhi[24, x : x + 1], v_col[32 * x : 32 * x + 32]
            )
            coef[0, x] = 0.05 - 0.5 * after
            coef[1, x] = 0.05 + 0.5 * before
            coef[2, x] = 0.05 - 0.5 * y_next
            coef[3, x] = 0.05 + 0.5 * y_prev
            coef[4, x] = 0.05 - 0.5 * z_next
            coef[5, x] = 0.05 + 0.5 * z_prev

    zcol[...] = all_z_columns(zlo[0:GROUP, :], zhi[0:GROUP, :])
    for x in range(8):
        ce = [coef[i, x] for i in range(6)]
        for f in range(GROUP):
            centre = q[f, x]
            before = xlo[f].astype(F32) if x == 0 else q[f, x - 1]
            after = xhi[f].astype(F32) if x == 7 else q[f, x + 1]
            z_col = zcol[32 * x : 32 * x + 32, 128 * f : 128 * f + 128]
            y_next, y_prev, z_next, z_prev = shifted(centre, ylo[f, x : x + 1], yhi[f, x : x + 1], z_col)
            moved = (
                0.7 * centre
                + (ce[0] * after + ce[1] * before)
                + (ce[2] * y_next + ce[3] * y_prev)
                + (ce[4] * z_next + ce[5] * z_prev)
            )
            if kind == 1:
                new = moved
            elif kind == 2:
                new = 0.75 * start[f, x] + 0.25 * moved
            else:
                new = (1.0 / 3.0) * start[f, x] + (2.0 / 3.0) * moved
            out[f, x] = new
            if kind < 3:
                put_faces(new, f, x, xf, xl, yf, yl)
    if kind < 3:
        for f in range(GROUP):
            put_z_faces(out, f, zf, zl)


def diffuse_kernel(rates, q, xlo, xhi, ylo, yhi, zlo, zhi, heats, out, activity, zcol):
    @pl.when(pl.program_id(0) == 0)
    def _():
        activity[0, 0] = jnp.sum(heats[...]) * (1.0 / (8.0 * 128.0))

    zcol[...] = all_z_columns(zlo[...], zhi[...])
    for f in range(LAST_GROUP):
        rate = rates[pl.program_id(0) * LAST_GROUP + f]
        for x in range(8):
            centre = q[f, x]
            before = xlo[f].astype(F32) if x == 0 else q[f, x - 1]
            after = xhi[f].astype(F32) if x == 7 else q[f, x + 1]
            z_col = zcol[32 * x : 32 * x + 32, 128 * f : 128 * f + 128]
            y_next, y_prev, z_next, z_prev = shifted(centre, ylo[f, x : x + 1], yhi[f, x : x + 1], z_col)
            spread = (after + before) + (y_next + y_prev) + (z_next + z_prev) - 6.0 * centre
            out[f, x] = centre + rate * spread


def columns_kernel(w_in, b_in, w_mid, w_low, b_mid, b_low, b_out, w1, w2, w3, b2, b3, b4):
    bias = 0.5 * b_in[...]
    parts = []
    for _ in range(3):
        parts.append(bias.astype(BF16).astype(F32))
        bias = bias - parts[-1]
    zeros = jnp.zeros((5, bias.shape[1]), F32)
    w1[...] = jnp.concatenate([0.5 * w_in[...].astype(F32), *parts, zeros], axis=0).T.astype(BF16)
    w2[...] = (0.5 * w_mid[...].astype(F32)).astype(BF16)
    w3[...] = (0.5 * w_low[...].astype(F32)).astype(BF16)
    for row, out, factor in (
        (b_mid, b2, 0.5),
        (b_low, b3, 0.5),
        (b_out, b4, 1.0),
    ):
        out[...] = jnp.broadcast_to(factor * row[...], (128, row.shape[1])).T


def network_kernel(listed, flowed, owned_by, w1, w2, w3, b2, b3, b4, w4, out, sent, xf, xl, yf, yl, zf, zl, heat):
    def copy(part, carry):
        rows = pl.ds(pl.multiple_of(part * 1536, 1536), 1536)
        out[rows, :] = flowed[rows, :]
        return carry

    def block(i):
        return jnp.where(listed[0, i] < 0, listed[0, 0], listed[0, i])

    def product(weights, cells):
        return jnp.dot(weights[...], cells, preferred_element_type=F32)

    def beside(bias):
        return jnp.concatenate([bias[...]] * TOGETHER, axis=1)

    def silu(half):
        return (half + half * jnp.tanh(half)).astype(BF16)

    def react(step, carry):
        first = step * TOGETHER
        rows = [pl.ds(block(first + j), 24, stride=256) for j in range(TOGETHER)]
        before = [flowed[r, :] for r in rows]
        ones = jnp.ones((8, TOGETHER * 128), F32)
        cells = jnp.concatenate([jnp.concatenate(before, axis=1), ones], axis=0).astype(BF16)
        hidden = silu(product(w1, cells))
        hidden = silu(product(w2, hidden) + beside(b2))
        hidden = silu(product(w3, hidden) + beside(b3))
        result = product(w4, hidden) + beside(b4)
        for j in range(TOGETHER):
            increment = result[:, 128 * j : 128 * j + 128]
            out[rows[j], :] = before[j] + increment
            heat[pl.ds(first + j, 1), :] = increment[0:1] * increment[0:1]
        return carry

    def faces(part, carry):
        ends = z_ends(out[pl.ds(pl.multiple_of(part * 1536, 1536), 1536), :])
        for j in range(6):
            f = 6 * part + j
            base = pl.multiple_of(256 * f, 256)
            xf[f] = out[pl.ds(base, 32), :].astype(BF16)
            xl[f] = out[pl.ds(base + 224, 32), :].astype(BF16)
            yf[f] = out[pl.ds(base, 8, stride=32), :]
            yl[f] = out[pl.ds(base + 31, 8, stride=32), :]
            zf[pl.ds(f, 1), :] = ends[0:1, 256 * j : 256 * j + 256]
            zl[pl.ds(f, 1), :] = ends[1:2, 256 * j : 256 * j + 256]
        return carry

    heat[...] = jnp.zeros_like(heat)
    lax.fori_loop(0, 4, copy, 0)
    count = lax.fori_loop(0, LISTED, lambda i, n: n + jnp.where(listed[0, i] < 0, 0, 1), 0)
    lax.fori_loop(0, (count + TOGETHER - 1) // TOGETHER, react, 0)
    lax.fori_loop(0, 4, faces, 0)
    sent[...] = jnp.dot(
        owned_by[...], heat[...], preferred_element_type=F32, precision=lax.Precision.HIGHEST
    )


def params(mib):
    return pltpu.CompilerParams(vmem_limit_bytes=mib * 1024 * 1024)


def sds(shape, dtype):
    return jax.ShapeDtypeStruct(shape, dtype)


IN_VMEM = pl.BlockSpec(memory_space=pltpu.VMEM)


def face_shapes(count):
    return [
        sds((count, 32, 128), BF16),
        sds((count, 32, 128), BF16),
        sds((count, 8, 128), F32),
        sds((count, 8, 128), F32),
        sds((count, 256), F32),
        sds((count, 256), F32),
    ]


def exchange(faces, axes=ALL):
    got = []
    for axis, first, last in zip(axes, faces[0::2], faces[1::2]):
        n = lax.axis_size(axis)
        got.append(lax.ppermute(last, axis, [(i, (i + 1) % n) for i in range(n)]))
        got.append(lax.ppermute(first, axis, [((i + 1) % n, i) for i in range(n)]))
    return got


def section(kind, args, out_shapes):
    return pl.pallas_call(
        functools.partial(section_kernel, kind),
        in_specs=[IN_VMEM] * len(args),
        out_specs=[IN_VMEM] * len(out_shapes),
        out_shape=out_shapes,
        scratch_shapes=[pltpu.VMEM((256, 128 * GROUP), F32)],
        compiler_params=params(24),
    )(*args)


def swap(tiles):
    return lax.all_to_all(tiles, ALL, split_axis=0, concat_axis=0, tiled=True)


def local(
    fields,
    velocity,
    diffusivity,
    weight_in,
    bias_in,
    weight_mid,
    bias_mid,
    weight_low,
    bias_low,
    weight_out,
    bias_out,
    react_list,
    owner_table,
):
    brick = sds(fields.shape, F32)
    owners = owner_table[0]
    owned_by = (owners[None, :] == jnp.arange(128, dtype=jnp.int32)[:, None]).astype(F32)

    x_faces = pl.pallas_call(
        x_faces_kernel,
        in_specs=[pl.BlockSpec(memory_space=pltpu.HBM)] * 2,
        out_specs=[IN_VMEM] * 2,
        out_shape=face_shapes(25)[:2],
        scratch_shapes=[pltpu.VMEM((2, 25, 32, 128), F32), pltpu.SemaphoreType.DMA((2, 2))],
        compiler_params=params(58),
    )(fields, velocity)
    more_faces = pl.pallas_call(
        prep_kernel, out_shape=face_shapes(25)[2:], compiler_params=params(24)
    )(fields, velocity)
    halo = exchange(x_faces, ALL[:1]) + exchange(more_faces, ALL[1:])
    one, coef, *faces = section(
        1, (fields, *halo, velocity, *halo), [brick, sds((6, 8, 32, 128), F32), *face_shapes(24)]
    )
    one, *given = lax.optimization_barrier(
        (
            one,
            weight_in,
            bias_in.reshape(1, -1),
            weight_mid.T,
            weight_low.T,
            *(b.reshape(1, -1) for b in (bias_mid, bias_low, bias_out)),
        )
    )
    columns = pl.pallas_call(
        columns_kernel,
        out_shape=[
            sds((weight_in.shape[1], 32), BF16),
            sds(weight_mid.shape[::-1], BF16),
            sds(weight_low.shape[::-1], BF16),
            *(sds((b.shape[0], 128), F32) for b in (bias_mid, bias_low, bias_out)),
        ],
        compiler_params=params(20),
        cost_estimate=pl.CostEstimate(flops=0, bytes_accessed=8 * 2**20, transcendentals=0),
    )(*given)
    two, *faces = section(2, (one, fields, *exchange(faces), coef), [brick, *face_shapes(24)])
    (flowed,) = section(3, (two, fields, *exchange(faces), coef), [brick])
    reacted, sent, *faces = pl.pallas_call(
        network_kernel,
        in_specs=[pl.BlockSpec(memory_space=pltpu.SMEM)] + [IN_VMEM] * 9,
        out_specs=[IN_VMEM] * 8,
        out_shape=[sds((24 * 256, 128), F32), sds((128, 128), F32), *face_shapes(24)],
        scratch_shapes=[pltpu.VMEM((LISTED, 128), F32)],
        compiler_params=params(NETWORK_MIB),
    )(react_list, flowed.reshape(24 * 256, 128), owned_by, *columns, weight_out.T)
    reacted = reacted.reshape(fields.shape)
    around = exchange(faces)
    heats = swap(sent.reshape(128, 1, 128)).reshape(128, 128)
    part = LAST_GROUP
    bricks = pl.BlockSpec((part, 8, 32, 128), lambda g: (g, 0, 0, 0))
    x_part = pl.BlockSpec((part, 32, 128), lambda g: (g, 0, 0))
    y_part = pl.BlockSpec((part, 8, 128), lambda g: (g, 0, 0))
    z_part = pl.BlockSpec((part, 256), lambda g: (g, 0))
    smem = pl.BlockSpec(memory_space=pltpu.SMEM)
    updated, activity = pl.pallas_call(
        diffuse_kernel,
        grid=(24 // part,),
        in_specs=[smem, bricks, x_part, x_part, y_part, y_part, z_part, z_part]
        + [pl.BlockSpec((128, 128), lambda g: (0, 0))],
        out_specs=[bricks, smem],
        out_shape=[brick, sds((1, 1), F32)],
        scratch_shapes=[pltpu.VMEM((256, 128 * part), F32)],
        compiler_params=params(32),
        cost_estimate=pl.CostEstimate(flops=10**9, bytes_accessed=24 * 2**20, transcendentals=0),
    )(diffusivity, reacted, *around, heats)
    return (updated, activity.reshape(1))


def solution(mesh):
    return jax.shard_map(
        local,
        mesh=mesh,
        in_specs=(
            P(None, *ALL),
            P(None, *ALL),
            *(P(),) * 9,
            P(ALL, None),
            P(ALL, None),
        ),
        out_specs=(P(None, *ALL), P(ALL)),
        check_vma=False,
    )
```

```python
import functools

import jax
import jax.numpy as jnp
from jax import lax
from jax.experimental import pallas as pl
from jax.experimental.pallas import tpu as pltpu
from jax.sharding import PartitionSpec as P

GROUP = 24
LAST_GROUP = 8
TOGETHER = 12
LISTED = 96
NETWORK_MIB = 38
ALL = ("gx", "gy", "gz")
F32, BF16 = jnp.float32, jnp.bfloat16
TN = (((0,), (0,)), ((), ()))
NT = (((1,), (1,)), ((), ()))


def one_hot_ends():
    rows = lax.broadcasted_iota(jnp.int32, (16, 128), 0)
    lanes = lax.broadcasted_iota(jnp.int32, (16, 128), 1)
    return (((rows == 0) & (lanes == 0)) | ((rows == 1) & (lanes == 127))).astype(F32).astype(BF16)


def z_columns(low, high):
    rows = lax.broadcasted_iota(jnp.int32, (16, 256), 0)
    pair = jnp.where(rows == 0, low, jnp.where(rows == 1, high, 0.0)).astype(BF16)
    return lax.dot_general(pair, one_hot_ends(), TN, preferred_element_type=F32)


def all_z_columns(low, high):
    n = low.shape[0]
    rows = lax.broadcasted_iota(jnp.int32, (2 * n, 128 * n), 0)
    lanes = lax.broadcasted_iota(jnp.int32, (2 * n, 128 * n), 1)
    place = jnp.where(rows < n, 128 * rows, 128 * (rows - n) + 127)
    ends = (lanes == place).astype(F32).astype(BF16)
    pairs = jnp.concatenate([low, high], axis=0).astype(BF16)
    return lax.dot_general(pairs, ends, TN, preferred_element_type=F32)


def z_ends(cells):
    return lax.dot_general(one_hot_ends(), cells.astype(BF16), NT, preferred_element_type=F32)


def shifted(centre, y_low, y_high, z_col):
    rows = lax.broadcasted_iota(jnp.int32, (32, 128), 0)
    lanes = lax.broadcasted_iota(jnp.int32, (32, 128), 1)
    y_next = jnp.where(rows == 31, y_high, pltpu.roll(centre, 31, 0))
    y_prev = jnp.where(rows == 0, y_low, pltpu.roll(centre, 1, 0))
    z_next = jnp.where(lanes == 127, z_col, pltpu.roll(centre, 127, 1))
    z_prev = jnp.where(lanes == 0, z_col, pltpu.roll(centre, 1, 1))
    return y_next, y_prev, z_next, z_prev


def put_faces(new, f, x, xf, xl, yf, yl):
    if x == 0:
        xf[f] = new.astype(BF16)
    if x == 7:
        xl[f] = new.astype(BF16)
    yf[f, x : x + 1] = new[0:1]
    yl[f, x : x + 1] = new[31:32]


def put_z_faces(out, f, zf, zl):
    ends = z_ends(out[f].reshape(256, 128))
    zf[f : f + 1] = ends[0:1]
    zl[f : f + 1] = ends[1:2]


def x_faces_kernel(fields, velocity, xf, xl, planes, sems):
    copies = []
    for i, x in enumerate((0, 7)):
        copies.append(pltpu.make_async_copy(fields.at[:, x], planes.at[i, 0:24], sems.at[i, 0]))
        copies.append(pltpu.make_async_copy(velocity.at[0, x], planes.at[i, 24], sems.at[i, 1]))
    for copy in copies:
        copy.start()
    for copy in copies:
        copy.wait()
    xf[...] = planes[0].astype(BF16)
    xl[...] = planes[1].astype(BF16)


def prep_kernel(fields, velocity, yf, yl, zf, zl):
    for f in range(25):
        for x in range(8):
            cells = velocity[1, x] if f == 24 else fields[f, x]
            yf[f, x : x + 1] = cells[0:1]
            yl[f, x : x + 1] = cells[31:32]
        lines = velocity[2] if f == 24 else fields[f]
        ends = z_ends(lines.reshape(256, 128))
        zf[f : f + 1] = ends[0:1]
        zl[f : f + 1] = ends[1:2]


def section_kernel(kind, *refs):
    refs = list(refs)
    q = refs.pop(0)
    start = q if kind == 1 else refs.pop(0)
    xlo, xhi, ylo, yhi, zlo, zhi = refs[:6]
    del refs[:6]
    if kind == 1:
        velocity, vxlo, vxhi, vylo, vyhi, vzlo, vzhi = refs[:7]
        del refs[:7]
    else:
        coef = refs.pop(0)
    out = refs.pop(0)
    if kind == 1:
        coef = refs.pop(0)
    if kind < 3:
        xf, xl, yf, yl, zf, zl = refs[:6]
        del refs[:6]
    zcol = refs.pop(0)

    if kind == 1:
        v_col = z_columns(vzlo[24:25], vzhi[24:25])
        for x in range(8):
            before = vxlo[24].astype(F32) if x == 0 else velocity[0, x - 1]
            after = vxhi[24].astype(F32) if x == 7 else velocity[0, x + 1]
            y_next, y_prev, _, _ = shifted(
                velocity[1, x], vylo[24, x : x + 1], vyhi[24, x : x + 1], velocity[1, x]
            )
            _, _, z_next, z_prev = shifted(
                velocity[2, x], vylo[24, x : x + 1], vyhi[24, x : x + 1], v_col[32 * x : 32 * x + 32]
            )
            coef[0, x] = 0.05 - 0.5 * after
            coef[1, x] = 0.05 + 0.5 * before
            coef[2, x] = 0.05 - 0.5 * y_next
            coef[3, x] = 0.05 + 0.5 * y_prev
            coef[4, x] = 0.05 - 0.5 * z_next
            coef[5, x] = 0.05 + 0.5 * z_prev

    zcol[...] = all_z_columns(zlo[0:GROUP, :], zhi[0:GROUP, :])
    for x in range(8):
        ce = [coef[i, x] for i in range(6)]
        for f in range(GROUP):
            centre = q[f, x]
            before = xlo[f].astype(F32) if x == 0 else q[f, x - 1]
            after = xhi[f].astype(F32) if x == 7 else q[f, x + 1]
            z_col = zcol[32 * x : 32 * x + 32, 128 * f : 128 * f + 128]
            y_next, y_prev, z_next, z_prev = shifted(centre, ylo[f, x : x + 1], yhi[f, x : x + 1], z_col)
            moved = (
                0.7 * centre
                + (ce[0] * after + ce[1] * before)
                + (ce[2] * y_next + ce[3] * y_prev)
                + (ce[4] * z_next + ce[5] * z_prev)
            )
            if kind == 1:
                new = moved
            elif kind == 2:
                new = 0.75 * start[f, x] + 0.25 * moved
            else:
                new = (1.0 / 3.0) * start[f, x] + (2.0 / 3.0) * moved
            out[f, x] = new
            if kind < 3:
                put_faces(new, f, x, xf, xl, yf, yl)
    if kind < 3:
        for f in range(GROUP):
            put_z_faces(out, f, zf, zl)


def activity_kernel(heats, activity):
    activity[0, 0] = jnp.sum(heats[...]) * (1.0 / (8.0 * 128.0))


def diffuse_kernel(rates, q, xlo, xhi, ylo, yhi, zlo, zhi, out, zcol):
    zcol[...] = all_z_columns(zlo[...], zhi[...])
    for f in range(LAST_GROUP):
        rate = rates[pl.program_id(0) * LAST_GROUP + f]
        for x in range(8):
            centre = q[f, x]
            before = xlo[f].astype(F32) if x == 0 else q[f, x - 1]
            after = xhi[f].astype(F32) if x == 7 else q[f, x + 1]
            z_col = zcol[32 * x : 32 * x + 32, 128 * f : 128 * f + 128]
            y_next, y_prev, z_next, z_prev = shifted(centre, ylo[f, x : x + 1], yhi[f, x : x + 1], z_col)
            spread = (after + before) + (y_next + y_prev) + (z_next + z_prev) - 6.0 * centre
            out[f, x] = centre + rate * spread


def columns_kernel(w_in, b_in, w_mid, w_low, b_mid, b_low, b_out, w1, w2, w3, b2, b3, b4):
    bias = 0.5 * b_in[...]
    parts = []
    for _ in range(3):
        parts.append(bias.astype(BF16).astype(F32))
        bias = bias - parts[-1]
    zeros = jnp.zeros((5, bias.shape[1]), F32)
    w1[...] = jnp.concatenate([0.5 * w_in[...].astype(F32), *parts, zeros], axis=0).T.astype(BF16)
    w2[...] = (0.5 * w_mid[...].astype(F32)).astype(BF16)
    w3[...] = (0.5 * w_low[...].astype(F32)).astype(BF16)
    for row, out, factor in (
        (b_mid, b2, 0.5),
        (b_low, b3, 0.5),
        (b_out, b4, 1.0),
    ):
        out[...] = jnp.broadcast_to(factor * row[...], (128, row.shape[1])).T


def network_kernel(listed, flowed, owned_by, w1, w2, w3, b2, b3, b4, w4, out, sent, xf, xl, yf, yl, zf, zl, heat):
    def copy(part, carry):
        rows = pl.ds(pl.multiple_of(part * 1536, 1536), 1536)
        out[rows, :] = flowed[rows, :]
        return carry

    def block(i):
        return jnp.where(listed[0, i] < 0, listed[0, 0], listed[0, i])

    def product(weights, cells):
        return jnp.dot(weights[...], cells, preferred_element_type=F32)

    def beside(bias):
        return jnp.concatenate([bias[...]] * TOGETHER, axis=1)

    def silu(half):
        return (half + half * jnp.tanh(half)).astype(BF16)

    def react(step, carry):
        first = step * TOGETHER
        rows = [pl.ds(block(first + j), 24, stride=256) for j in range(TOGETHER)]
        before = [flowed[r, :] for r in rows]
        ones = jnp.ones((8, TOGETHER * 128), F32)
        cells = jnp.concatenate([jnp.concatenate(before, axis=1), ones], axis=0).astype(BF16)
        hidden = silu(product(w1, cells))
        hidden = silu(product(w2, hidden) + beside(b2))
        hidden = silu(product(w3, hidden) + beside(b3))
        result = product(w4, hidden) + beside(b4)
        for j in range(TOGETHER):
            increment = result[:, 128 * j : 128 * j + 128]
            out[rows[j], :] = before[j] + increment
            heat[pl.ds(first + j, 1), :] = increment[0:1] * increment[0:1]
        return carry

    def faces(part, carry):
        ends = z_ends(out[pl.ds(pl.multiple_of(part * 1536, 1536), 1536), :])
        for j in range(6):
            f = 6 * part + j
            base = pl.multiple_of(256 * f, 256)
            xf[f] = out[pl.ds(base, 32), :].astype(BF16)
            xl[f] = out[pl.ds(base + 224, 32), :].astype(BF16)
            yf[f] = out[pl.ds(base, 8, stride=32), :]
            yl[f] = out[pl.ds(base + 31, 8, stride=32), :]
            zf[pl.ds(f, 1), :] = ends[0:1, 256 * j : 256 * j + 256]
            zl[pl.ds(f, 1), :] = ends[1:2, 256 * j : 256 * j + 256]
        return carry

    heat[...] = jnp.zeros_like(heat)
    lax.fori_loop(0, 4, copy, 0)
    count = lax.fori_loop(0, LISTED, lambda i, n: n + jnp.where(listed[0, i] < 0, 0, 1), 0)
    lax.fori_loop(0, (count + TOGETHER - 1) // TOGETHER, react, 0)
    lax.fori_loop(0, 4, faces, 0)
    sent[...] = jnp.dot(
        owned_by[...], heat[...], preferred_element_type=F32, precision=lax.Precision.HIGHEST
    )


def params(mib):
    return pltpu.CompilerParams(vmem_limit_bytes=mib * 1024 * 1024)


def sds(shape, dtype):
    return jax.ShapeDtypeStruct(shape, dtype)


IN_VMEM = pl.BlockSpec(memory_space=pltpu.VMEM)


def face_shapes(count):
    return [
        sds((count, 32, 128), BF16),
        sds((count, 32, 128), BF16),
        sds((count, 8, 128), F32),
        sds((count, 8, 128), F32),
        sds((count, 256), F32),
        sds((count, 256), F32),
    ]


def exchange(faces, axes=ALL):
    got = []
    for axis, first, last in zip(axes, faces[0::2], faces[1::2]):
        n = lax.axis_size(axis)
        got.append(lax.ppermute(last, axis, [(i, (i + 1) % n) for i in range(n)]))
        got.append(lax.ppermute(first, axis, [((i + 1) % n, i) for i in range(n)]))
    return got


def section(kind, args, out_shapes):
    return pl.pallas_call(
        functools.partial(section_kernel, kind),
        in_specs=[IN_VMEM] * len(args),
        out_specs=[IN_VMEM] * len(out_shapes),
        out_shape=out_shapes,
        scratch_shapes=[pltpu.VMEM((256, 128 * GROUP), F32)],
        compiler_params=params(24),
    )(*args)


def swap(tiles):
    return lax.all_to_all(tiles, ALL, split_axis=0, concat_axis=0, tiled=True)


def local(
    fields,
    velocity,
    diffusivity,
    weight_in,
    bias_in,
    weight_mid,
    bias_mid,
    weight_low,
    bias_low,
    weight_out,
    bias_out,
    react_list,
    owner_table,
):
    brick = sds(fields.shape, F32)
    owners = owner_table[0]
    owned_by = (owners[None, :] == jnp.arange(128, dtype=jnp.int32)[:, None]).astype(F32)

    x_faces = pl.pallas_call(
        x_faces_kernel,
        in_specs=[pl.BlockSpec(memory_space=pltpu.HBM)] * 2,
        out_specs=[IN_VMEM] * 2,
        out_shape=face_shapes(25)[:2],
        scratch_shapes=[pltpu.VMEM((2, 25, 32, 128), F32), pltpu.SemaphoreType.DMA((2, 2))],
        compiler_params=params(58),
    )(fields, velocity)
    more_faces = pl.pallas_call(
        prep_kernel, out_shape=face_shapes(25)[2:], compiler_params=params(24)
    )(fields, velocity)
    halo = exchange(x_faces, ALL[:1]) + exchange(more_faces, ALL[1:])
    one, coef, *faces = section(
        1, (fields, *halo, velocity, *halo), [brick, sds((6, 8, 32, 128), F32), *face_shapes(24)]
    )
    one, *given = lax.optimization_barrier(
        (
            one,
            weight_in,
            bias_in.reshape(1, -1),
            weight_mid.T,
            weight_low.T,
            *(b.reshape(1, -1) for b in (bias_mid, bias_low, bias_out)),
        )
    )
    columns = pl.pallas_call(
        columns_kernel,
        out_shape=[
            sds((weight_in.shape[1], 32), BF16),
            sds(weight_mid.shape[::-1], BF16),
            sds(weight_low.shape[::-1], BF16),
            *(sds((b.shape[0], 128), F32) for b in (bias_mid, bias_low, bias_out)),
        ],
        compiler_params=params(20),
        cost_estimate=pl.CostEstimate(flops=0, bytes_accessed=8 * 2**20, transcendentals=0),
    )(*given)
    two, *faces = section(2, (one, fields, *exchange(faces), coef), [brick, *face_shapes(24)])
    (flowed,) = section(3, (two, fields, *exchange(faces), coef), [brick])
    reacted, sent, *faces = pl.pallas_call(
        network_kernel,
        in_specs=[pl.BlockSpec(memory_space=pltpu.SMEM)] + [IN_VMEM] * 9,
        out_specs=[IN_VMEM] * 8,
        out_shape=[sds((24 * 256, 128), F32), sds((128, 128), F32), *face_shapes(24)],
        scratch_shapes=[pltpu.VMEM((LISTED, 128), F32)],
        compiler_params=params(NETWORK_MIB),
    )(react_list, flowed.reshape(24 * 256, 128), owned_by, *columns, weight_out.T)
    reacted = reacted.reshape(fields.shape)
    x_and_y = exchange(faces[:4])
    *z_faces, x_and_y[0], x_and_y[1] = lax.optimization_barrier((*faces[4:], *x_and_y[:2]))
    around = x_and_y + exchange(z_faces, ALL[2:])
    heats = swap(sent.reshape(128, 1, 128)).reshape(128, 128)
    part = LAST_GROUP
    bricks = pl.BlockSpec((part, 8, 32, 128), lambda g: (g, 0, 0, 0))
    x_part = pl.BlockSpec((part, 32, 128), lambda g: (g, 0, 0))
    y_part = pl.BlockSpec((part, 8, 128), lambda g: (g, 0, 0))
    z_part = pl.BlockSpec((part, 256), lambda g: (g, 0))
    smem = pl.BlockSpec(memory_space=pltpu.SMEM)
    updated = pl.pallas_call(
        diffuse_kernel,
        grid=(24 // part,),
        in_specs=[smem, bricks, x_part, x_part, y_part, y_part, z_part, z_part],
        out_specs=bricks,
        out_shape=brick,
        scratch_shapes=[pltpu.VMEM((256, 128 * part), F32)],
        compiler_params=params(32),
        cost_estimate=pl.CostEstimate(flops=10**7, bytes_accessed=6 * 2**20, transcendentals=0),
    )(diffusivity, reacted, *around)
    heats, updated = lax.optimization_barrier((heats, updated))
    activity = pl.pallas_call(activity_kernel, out_specs=smem, out_shape=sds((1, 1), F32))(heats)
    return (updated, activity.reshape(1))


def solution(mesh):
    return jax.shard_map(
        local,
        mesh=mesh,
        in_specs=(
            P(None, *ALL),
            P(None, *ALL),
            *(P(),) * 9,
            P(ALL, None),
            P(ALL, None),
        ),
        out_specs=(P(None, *ALL), P(ALL)),
        check_vma=False,
    )
```

```python
import functools

import jax
import jax.numpy as jnp
from jax import lax
from jax.experimental import pallas as pl
from jax.experimental.pallas import tpu as pltpu
from jax.sharding import PartitionSpec as P

GROUP = 24
LAST_GROUP = 8
TOGETHER = 16
LISTED = 96
NETWORK_MIB = 42
ALL = ("gx", "gy", "gz")
F32, BF16 = jnp.float32, jnp.bfloat16
TN = (((0,), (0,)), ((), ()))
NT = (((1,), (1,)), ((), ()))


def one_hot_ends():
    rows = lax.broadcasted_iota(jnp.int32, (16, 128), 0)
    lanes = lax.broadcasted_iota(jnp.int32, (16, 128), 1)
    return (((rows == 0) & (lanes == 0)) | ((rows == 1) & (lanes == 127))).astype(F32).astype(BF16)


def z_columns(low, high):
    rows = lax.broadcasted_iota(jnp.int32, (16, 256), 0)
    pair = jnp.where(rows == 0, low, jnp.where(rows == 1, high, 0.0)).astype(BF16)
    return lax.dot_general(pair, one_hot_ends(), TN, preferred_element_type=F32)


def all_z_columns(low, high):
    n = low.shape[0]
    rows = lax.broadcasted_iota(jnp.int32, (2 * n, 128 * n), 0)
    lanes = lax.broadcasted_iota(jnp.int32, (2 * n, 128 * n), 1)
    place = jnp.where(rows < n, 128 * rows, 128 * (rows - n) + 127)
    ends = (lanes == place).astype(F32).astype(BF16)
    pairs = jnp.concatenate([low, high], axis=0).astype(BF16)
    return lax.dot_general(pairs, ends, TN, preferred_element_type=F32)


def z_ends(cells):
    return lax.dot_general(one_hot_ends(), cells.astype(BF16), NT, preferred_element_type=F32)


def shifted(centre, y_low, y_high, z_col):
    rows = lax.broadcasted_iota(jnp.int32, (32, 128), 0)
    lanes = lax.broadcasted_iota(jnp.int32, (32, 128), 1)
    y_next = jnp.where(rows == 31, y_high, pltpu.roll(centre, 31, 0))
    y_prev = jnp.where(rows == 0, y_low, pltpu.roll(centre, 1, 0))
    z_next = jnp.where(lanes == 127, z_col, pltpu.roll(centre, 127, 1))
    z_prev = jnp.where(lanes == 0, z_col, pltpu.roll(centre, 1, 1))
    return y_next, y_prev, z_next, z_prev


def put_faces(new, f, x, xf, xl, yf, yl):
    if x == 0:
        xf[f] = new.astype(BF16)
    if x == 7:
        xl[f] = new.astype(BF16)
    yf[f, x : x + 1] = new[0:1]
    yl[f, x : x + 1] = new[31:32]


def put_z_faces(out, f, zf, zl):
    ends = z_ends(out[f].reshape(256, 128))
    zf[f : f + 1] = ends[0:1]
    zl[f : f + 1] = ends[1:2]


def x_faces_kernel(fields, velocity, xf, xl, planes, sems):
    copies = []
    for i, x in enumerate((0, 7)):
        copies.append(pltpu.make_async_copy(fields.at[:, x], planes.at[i, 0:24], sems.at[i, 0]))
        copies.append(pltpu.make_async_copy(velocity.at[0, x], planes.at[i, 24], sems.at[i, 1]))
    for copy in copies:
        copy.start()
    for copy in copies:
        copy.wait()
    xf[...] = planes[0].astype(BF16)
    xl[...] = planes[1].astype(BF16)


def prep_kernel(fields, velocity, yf, yl, zf, zl):
    for f in range(25):
        for x in range(8):
            cells = velocity[1, x] if f == 24 else fields[f, x]
            yf[f, x : x + 1] = cells[0:1]
            yl[f, x : x + 1] = cells[31:32]
        lines = velocity[2] if f == 24 else fields[f]
        ends = z_ends(lines.reshape(256, 128))
        zf[f : f + 1] = ends[0:1]
        zl[f : f + 1] = ends[1:2]


def section_kernel(kind, *refs):
    refs = list(refs)
    q = refs.pop(0)
    start = q if kind == 1 else refs.pop(0)
    xlo, xhi, ylo, yhi, zlo, zhi = refs[:6]
    del refs[:6]
    if kind == 1:
        velocity, vxlo, vxhi, vylo, vyhi, vzlo, vzhi = refs[:7]
        del refs[:7]
    else:
        coef = refs.pop(0)
    out = refs.pop(0)
    if kind == 1:
        coef = refs.pop(0)
    if kind < 3:
        xf, xl, yf, yl, zf, zl = refs[:6]
        del refs[:6]
    zcol = refs.pop(0)

    if kind == 1:
        v_col = z_columns(vzlo[24:25], vzhi[24:25])
        for x in range(8):
            before = vxlo[24].astype(F32) if x == 0 else velocity[0, x - 1]
            after = vxhi[24].astype(F32) if x == 7 else velocity[0, x + 1]
            y_next, y_prev, _, _ = shifted(
                velocity[1, x], vylo[24, x : x + 1], vyhi[24, x : x + 1], velocity[1, x]
            )
            _, _, z_next, z_prev = shifted(
                velocity[2, x], vylo[24, x : x + 1], vyhi[24, x : x + 1], v_col[32 * x : 32 * x + 32]
            )
            coef[0, x] = 0.05 - 0.5 * after
            coef[1, x] = 0.05 + 0.5 * before
            coef[2, x] = 0.05 - 0.5 * y_next
            coef[3, x] = 0.05 + 0.5 * y_prev
            coef[4, x] = 0.05 - 0.5 * z_next
            coef[5, x] = 0.05 + 0.5 * z_prev

    zcol[...] = all_z_columns(zlo[0:GROUP, :], zhi[0:GROUP, :])
    for x in range(8):
        ce = [coef[i, x] for i in range(6)]
        for f in range(GROUP):
            centre = q[f, x]
            before = xlo[f].astype(F32) if x == 0 else q[f, x - 1]
            after = xhi[f].astype(F32) if x == 7 else q[f, x + 1]
            z_col = zcol[32 * x : 32 * x + 32, 128 * f : 128 * f + 128]
            y_next, y_prev, z_next, z_prev = shifted(centre, ylo[f, x : x + 1], yhi[f, x : x + 1], z_col)
            moved = (
                0.7 * centre
                + (ce[0] * after + ce[1] * before)
                + (ce[2] * y_next + ce[3] * y_prev)
                + (ce[4] * z_next + ce[5] * z_prev)
            )
            if kind == 1:
                new = moved
            elif kind == 2:
                new = 0.75 * start[f, x] + 0.25 * moved
            else:
                new = (1.0 / 3.0) * start[f, x] + (2.0 / 3.0) * moved
            out[f, x] = new
            if kind < 3:
                put_faces(new, f, x, xf, xl, yf, yl)
    if kind < 3:
        for f in range(GROUP):
            put_z_faces(out, f, zf, zl)


def activity_kernel(heats, activity):
    activity[0, 0] = jnp.sum(heats[...]) * (1.0 / (8.0 * 128.0))


def diffuse_kernel(rates, q, xlo, xhi, ylo, yhi, zlo, zhi, out, zcol):
    zcol[...] = all_z_columns(zlo[...], zhi[...])
    for f in range(LAST_GROUP):
        rate = rates[pl.program_id(0) * LAST_GROUP + f]
        for x in range(8):
            centre = q[f, x]
            before = xlo[f].astype(F32) if x == 0 else q[f, x - 1]
            after = xhi[f].astype(F32) if x == 7 else q[f, x + 1]
            z_col = zcol[32 * x : 32 * x + 32, 128 * f : 128 * f + 128]
            y_next, y_prev, z_next, z_prev = shifted(centre, ylo[f, x : x + 1], yhi[f, x : x + 1], z_col)
            spread = (after + before) + (y_next + y_prev) + (z_next + z_prev) - 6.0 * centre
            out[f, x] = centre + rate * spread


def columns_kernel(w_in, b_in, w_mid, w_low, b_mid, b_low, b_out, w1, w2, w3, b2, b3, b4):
    bias = 0.5 * b_in[...]
    parts = []
    for _ in range(3):
        parts.append(bias.astype(BF16).astype(F32))
        bias = bias - parts[-1]
    zeros = jnp.zeros((5, bias.shape[1]), F32)
    w1[...] = jnp.concatenate([0.5 * w_in[...].astype(F32), *parts, zeros], axis=0).T.astype(BF16)
    w2[...] = (0.5 * w_mid[...].astype(F32)).astype(BF16)
    w3[...] = (0.5 * w_low[...].astype(F32)).astype(BF16)
    for row, out, factor in (
        (b_mid, b2, 0.5),
        (b_low, b3, 0.5),
        (b_out, b4, 1.0),
    ):
        out[...] = jnp.broadcast_to(factor * row[...], (128, row.shape[1])).T


def network_kernel(listed, flowed, owned_by, w1, w2, w3, b2, b3, b4, w4, out, sent, xf, xl, yf, yl, zf, zl, heat):
    def copy(part, carry):
        rows = pl.ds(pl.multiple_of(part * 1536, 1536), 1536)
        out[rows, :] = flowed[rows, :]
        return carry

    def block(i):
        return jnp.where(listed[0, i] < 0, listed[0, 0], listed[0, i])

    def product(weights, cells):
        return jnp.dot(weights[...], cells, preferred_element_type=F32)

    def beside(bias):
        return jnp.concatenate([bias[...]] * TOGETHER, axis=1)

    def silu(half):
        return (half + half * jnp.tanh(half)).astype(BF16)

    def react(step, carry):
        first = step * TOGETHER
        rows = [pl.ds(block(first + j), 24, stride=256) for j in range(TOGETHER)]
        before = [flowed[r, :] for r in rows]
        ones = jnp.ones((8, TOGETHER * 128), F32)
        cells = jnp.concatenate([jnp.concatenate(before, axis=1), ones], axis=0).astype(BF16)
        hidden = silu(product(w1, cells))
        hidden = silu(product(w2, hidden) + beside(b2))
        hidden = silu(product(w3, hidden) + beside(b3))
        result = product(w4, hidden) + beside(b4)
        for j in range(TOGETHER):
            increment = result[:, 128 * j : 128 * j + 128]
            out[rows[j], :] = before[j] + increment
            heat[pl.ds(first + j, 1), :] = increment[0:1] * increment[0:1]
        return carry

    def faces(part, carry):
        ends = z_ends(out[pl.ds(pl.multiple_of(part * 1536, 1536), 1536), :])
        for j in range(6):
            f = 6 * part + j
            base = pl.multiple_of(256 * f, 256)
            xf[f] = out[pl.ds(base, 32), :].astype(BF16)
            xl[f] = out[pl.ds(base + 224, 32), :].astype(BF16)
            yf[f] = out[pl.ds(base, 8, stride=32), :]
            yl[f] = out[pl.ds(base + 31, 8, stride=32), :]
            zf[pl.ds(f, 1), :] = ends[0:1, 256 * j : 256 * j + 256]
            zl[pl.ds(f, 1), :] = ends[1:2, 256 * j : 256 * j + 256]
        return carry

    heat[...] = jnp.zeros_like(heat)
    lax.fori_loop(0, 4, copy, 0)
    count = lax.fori_loop(0, LISTED, lambda i, n: n + jnp.where(listed[0, i] < 0, 0, 1), 0)
    lax.fori_loop(0, (count + TOGETHER - 1) // TOGETHER, react, 0)
    lax.fori_loop(0, 4, faces, 0)
    sent[...] = jnp.dot(
        owned_by[...], heat[...], preferred_element_type=F32, precision=lax.Precision.HIGHEST
    )


def params(mib):
    return pltpu.CompilerParams(vmem_limit_bytes=mib * 1024 * 1024)


def sds(shape, dtype):
    return jax.ShapeDtypeStruct(shape, dtype)


IN_VMEM = pl.BlockSpec(memory_space=pltpu.VMEM)


def face_shapes(count):
    return [
        sds((count, 32, 128), BF16),
        sds((count, 32, 128), BF16),
        sds((count, 8, 128), F32),
        sds((count, 8, 128), F32),
        sds((count, 256), F32),
        sds((count, 256), F32),
    ]


def exchange(faces, axes=ALL):
    got = []
    for axis, first, last in zip(axes, faces[0::2], faces[1::2]):
        n = lax.axis_size(axis)
        got.append(lax.ppermute(last, axis, [(i, (i + 1) % n) for i in range(n)]))
        got.append(lax.ppermute(first, axis, [((i + 1) % n, i) for i in range(n)]))
    return got


def section(kind, args, out_shapes):
    return pl.pallas_call(
        functools.partial(section_kernel, kind),
        in_specs=[IN_VMEM] * len(args),
        out_specs=[IN_VMEM] * len(out_shapes),
        out_shape=out_shapes,
        scratch_shapes=[pltpu.VMEM((256, 128 * GROUP), F32)],
        compiler_params=params(24),
    )(*args)


def swap(tiles):
    return lax.all_to_all(tiles, ALL, split_axis=0, concat_axis=0, tiled=True)


def local(
    fields,
    velocity,
    diffusivity,
    weight_in,
    bias_in,
    weight_mid,
    bias_mid,
    weight_low,
    bias_low,
    weight_out,
    bias_out,
    react_list,
    owner_table,
):
    brick = sds(fields.shape, F32)
    owners = owner_table[0]
    owned_by = (owners[None, :] == jnp.arange(128, dtype=jnp.int32)[:, None]).astype(F32)

    x_faces = pl.pallas_call(
        x_faces_kernel,
        in_specs=[pl.BlockSpec(memory_space=pltpu.HBM)] * 2,
        out_specs=[IN_VMEM] * 2,
        out_shape=face_shapes(25)[:2],
        scratch_shapes=[pltpu.VMEM((2, 25, 32, 128), F32), pltpu.SemaphoreType.DMA((2, 2))],
        compiler_params=params(58),
    )(fields, velocity)
    more_faces = pl.pallas_call(
        prep_kernel, out_shape=face_shapes(25)[2:], compiler_params=params(24)
    )(fields, velocity)
    halo = exchange(x_faces, ALL[:1]) + exchange(more_faces, ALL[1:])
    one, coef, *faces = section(
        1, (fields, *halo, velocity, *halo), [brick, sds((6, 8, 32, 128), F32), *face_shapes(24)]
    )
    one, *given = lax.optimization_barrier(
        (
            one,
            weight_in,
            bias_in.reshape(1, -1),
            weight_mid.T,
            weight_low.T,
            *(b.reshape(1, -1) for b in (bias_mid, bias_low, bias_out)),
        )
    )
    columns = pl.pallas_call(
        columns_kernel,
        out_shape=[
            sds((weight_in.shape[1], 32), BF16),
            sds(weight_mid.shape[::-1], BF16),
            sds(weight_low.shape[::-1], BF16),
            *(sds((b.shape[0], 128), F32) for b in (bias_mid, bias_low, bias_out)),
        ],
        compiler_params=params(20),
        cost_estimate=pl.CostEstimate(flops=0, bytes_accessed=8 * 2**20, transcendentals=0),
    )(*given)
    two, *faces = section(2, (one, fields, *exchange(faces), coef), [brick, *face_shapes(24)])
    (flowed,) = section(3, (two, fields, *exchange(faces), coef), [brick])
    reacted, sent, *faces = pl.pallas_call(
        network_kernel,
        in_specs=[pl.BlockSpec(memory_space=pltpu.SMEM)] + [IN_VMEM] * 9,
        out_specs=[IN_VMEM] * 8,
        out_shape=[sds((24 * 256, 128), F32), sds((128, 128), F32), *face_shapes(24)],
        scratch_shapes=[pltpu.VMEM((LISTED, 128), F32)],
        compiler_params=params(NETWORK_MIB),
    )(react_list, flowed.reshape(24 * 256, 128), owned_by, *columns, weight_out.T)
    reacted = reacted.reshape(fields.shape)
    x_and_y = exchange(faces[:4])
    *z_faces, x_and_y[0], x_and_y[1] = lax.optimization_barrier((*faces[4:], *x_and_y[:2]))
    around = x_and_y + exchange(z_faces, ALL[2:])
    heats = swap(sent.reshape(128, 1, 128)).reshape(128, 128)
    part = LAST_GROUP
    bricks = pl.BlockSpec((part, 8, 32, 128), lambda g: (g, 0, 0, 0))
    x_part = pl.BlockSpec((part, 32, 128), lambda g: (g, 0, 0))
    y_part = pl.BlockSpec((part, 8, 128), lambda g: (g, 0, 0))
    z_part = pl.BlockSpec((part, 256), lambda g: (g, 0))
    smem = pl.BlockSpec(memory_space=pltpu.SMEM)
    updated = pl.pallas_call(
        diffuse_kernel,
        grid=(24 // part,),
        in_specs=[smem, bricks, x_part, x_part, y_part, y_part, z_part, z_part],
        out_specs=bricks,
        out_shape=brick,
        scratch_shapes=[pltpu.VMEM((256, 128 * part), F32)],
        compiler_params=params(32),
        cost_estimate=pl.CostEstimate(flops=10**7, bytes_accessed=6 * 2**20, transcendentals=0),
    )(diffusivity, reacted, *around)
    heats, updated = lax.optimization_barrier((heats, updated))
    activity = pl.pallas_call(activity_kernel, out_specs=smem, out_shape=sds((1, 1), F32))(heats)
    return (updated, activity.reshape(1))


def solution(mesh):
    return jax.shard_map(
        local,
        mesh=mesh,
        in_specs=(
            P(None, *ALL),
            P(None, *ALL),
            *(P(),) * 9,
            P(ALL, None),
            P(ALL, None),
        ),
        out_specs=(P(None, *ALL), P(ALL)),
        check_vma=False,
    )
```
